512 devices in a mesh: off: 64 (over y, x, z_lo), dep: 8 (over z_hi, core).
Axes of the slice: x: 4, y: 4, z: 16 (z_hi: 4, z_lo: 4; z = z_hi * 4 + z_lo), core: 2. Of those that a mesh axis runs over, the one named last changes fastest.
Arguments:
- snapshots: bfloat16 [64, 32, 64, 256], P('off', 'dep'), may hold values from -6 to 6
- reflect: bfloat16 [768, 32, 64, 256], P('off', 'dep'), may hold values from -0.21875 to 0.21875
- courant: float32 [32, 64, 256], P('dep'), may hold values from 0.03 to 0.18
- lags: int32 [768], P('off'), may hold values from -32 to 32, as said below
- owners: int32 [8], replicated, may hold values from 0 to 63, as said below
Outputs:
- scattered: float32 [32, 64, 256], P('dep')
The draws below stay inside these ranges and needn't reach their ends.
Inputs may be any that keep to these rules, and one draw needn't show every extreme that they name: `lags`: some offset has lag -32 and some offset has lag 32. `owners`: some step uses wavefield 0 and some step uses wavefield 64 - 1.
All inputs are finite; a program needn't handle non-finite values.
Results may differ from the reference program's by a relative error of at most 0.0003.
Values may be sent and summed in bfloat16 or wider, within the bound.
A program may use at most 64 MiB of HBM per device.

```python
import math
import jax
import jax.numpy as jnp
from jax import lax

NX = 256
NY = 64
ITERS = 8
LAG = 32
NOFF = 768
NZ = 32
NSNAP = 64


def draw_lags(key, part):
    first_key, second_key = jax.random.split(jax.random.fold_in(key, 17))
    values = jax.random.randint(first_key, (NOFF,), -LAG, LAG + 1)
    places = jax.random.permutation(second_key, NOFF)
    values = values.at[places[0]].set(-LAG).at[places[1]].set(LAG)
    return values.astype(jnp.int32)


def draw_owners(key, part):
    first_key, second_key = jax.random.split(jax.random.fold_in(key, 29))
    values = jax.random.randint(first_key, (ITERS,), 0, NSNAP)
    places = jax.random.permutation(second_key, ITERS)
    values = values.at[places[0]].set(0).at[places[1]].set(NSNAP - 1)
    return values.astype(jnp.int32)


def steps_of(rng, shape, pieces, smallest, high):
    def one(axis_at, shards_of):
        draws = jax.random.uniform(jax.random.fold_in(jax.random.fold_in(rng, 6), axis_at), (shards_of,), jnp.float32, smallest / len(pieces), high / len(pieces))
        return jnp.repeat(jnp.exp(draws), shape[axis_at] // shards_of).reshape((-1,) + (1,) * (len(shape) - axis_at - 1))

    factor_of = one(*pieces[0])
    for cut in pieces[1:]:
        factor_of = factor_of * one(*cut)
    return factor_of


def bell_draw(stream_key, extent, deviation, most, pieces=(), kind=jnp.bfloat16):
    level = steps_of(stream_key, extent, pieces, -0.22, 0.18) if pieces else 1.0
    drawn = jax.random.normal(stream_key, extent, jnp.float32) * deviation * level
    return jnp.minimum(jnp.maximum(drawn, -most), most).astype(kind)


def setup_inputs(seed: int = 0) -> dict:
    keys = jax.random.split(jax.random.key(seed), 6)
    return {
        "snapshots": bell_draw(keys[0], (NSNAP, NZ, NY, NX), 1.0, 6.0, ((0, 64), (1, 8))),
        "reflect": bell_draw(keys[1], (NOFF, NZ, NY, NX), NOFF ** -0.5, 0.21875, ((0, 64), (1, 8))),
        "courant": jnp.clip(jnp.exp(math.log(0.18) - 1.7917595 * jax.random.uniform(keys[2], (NZ, NY, NX), jnp.float32) ** steps_of(keys[2], (NZ, NY, NX), ((0, 8),), -0.2, 0.2)), 0.03, 0.18),
        "lags": draw_lags(jax.random.fold_in(keys[5], 71), 0),
        "owners": draw_owners(jax.random.fold_in(keys[5], 71), 0),
    }


STENCIL_WEIGHTS = (-205.0 / 72.0, 8.0 / 5.0, -1.0 / 5.0, 8.0 / 315.0, -1.0 / 560.0)


def stencil(padded, depth_cells, row_cells, column_cells):
    center = padded[4:4 + depth_cells, 4:4 + row_cells, 4:4 + column_cells]
    summed = (3.0 * STENCIL_WEIGHTS[0]) * center
    for distance in range(1, 5):
        neighbours = padded[4 + distance:4 + distance + depth_cells, 4:4 + row_cells, 4:4 + column_cells] + padded[4 - distance:4 - distance + depth_cells, 4:4 + row_cells, 4:4 + column_cells]
        neighbours = neighbours + padded[4:4 + depth_cells, 4 + distance:4 + distance + row_cells, 4:4 + column_cells] + padded[4:4 + depth_cells, 4 - distance:4 - distance + row_cells, 4:4 + column_cells]
        neighbours = neighbours + padded[4:4 + depth_cells, 4:4 + row_cells, 4 + distance:4 + distance + column_cells] + padded[4:4 + depth_cells, 4:4 + row_cells, 4 - distance:4 - distance + column_cells]
        summed = summed + STENCIL_WEIGHTS[distance] * neighbours
    return summed


def laplace(field):
    return stencil(jnp.pad(field, 4), field.shape[0], field.shape[1], field.shape[2])


def shifted_sum(reflect, acceleration, lags):
    width_cells = acceleration.shape[2]
    padded = jnp.pad(acceleration, ((0, 0), (0, 0), (LAG, LAG)))

    def add_offset(offset_index, summed):
        lag_now = lags[offset_index].astype(jnp.int32)
        window = lax.dynamic_slice_in_dim(padded, (LAG - lag_now).astype(jnp.int32), width_cells, 2)
        return summed + reflect[offset_index].astype(jnp.float32) * window

    return lax.fori_loop(0, reflect.shape[0], add_offset, jnp.zeros(acceleration.shape, acceleration.dtype))


def reference(snapshots, reflect, courant, lags, owners):
    scattered = jnp.zeros(courant.shape, courant.dtype)
    previous = jnp.zeros(courant.shape, courant.dtype)
    for step_now in range(ITERS):
        background = snapshots[owners[step_now]].astype(jnp.float32)
        acceleration = courant * laplace(background)
        source = shifted_sum(reflect, acceleration, lags)
        updated = 2.0 * scattered - previous + courant * laplace(scattered) + source
        previous = scattered
        scattered = updated
    return scattered
```

```python
import jax
import jax.numpy as jnp
from jax import lax
from jax.experimental import pallas as pl
from jax.experimental.pallas import tpu as pltpu
from jax.sharding import PartitionSpec as P

ITERS = 8
LAG = 32
WEIGHTS = (-205.0 / 72.0, 8.0 / 5.0, -1.0 / 5.0, 8.0 / 315.0, -1.0 / 560.0)
MESH = pl.DeviceIdType.MESH
F32 = jnp.float32
BF16 = jnp.bfloat16
OFFSETS = 12
CHUNKS = 3
PART = OFFSETS // CHUNKS


def rem(a, n):
    return lax.rem(a, jnp.int32(n))


def div(a, n):
    return lax.div(a, jnp.int32(n))


def block_of(xy):
    y, x = div(xy, 4), rem(xy, 4)
    return 4 * y + x + rem(y, 2) * (3 - 2 * x)


def column_of(block):
    return block_of(block)


def quarter_of(block, z):
    return z + rem(block, 2) * (3 - 2 * z)


def device_of(piece):
    block = div(piece, 4)
    return column_of(block) * 4 + quarter_of(block, rem(piece, 4))


def transposed(identity, matrix):
    return lax.dot_general(identity, matrix, (((1,), (1,)), ((), ())), preferred_element_type=F32)


def laplace(cur, left, right, up, down):
    row = lax.broadcasted_iota(jnp.int32, (8, 128), 0)
    lane = lax.broadcasted_iota(jnp.int32, (8, 128), 1)
    cell = rem(row, 4)
    line = rem(lane, 64)
    low = lane < 64
    turned = lambda v: pltpu.roll(v, 64, 1)
    swapped_cur = pltpu.roll(cur, 4, 0)
    ahead = jnp.where(row < 4, swapped_cur, pltpu.roll(down, 4, 0))
    behind = jnp.where(row >= 4, swapped_cur, pltpu.roll(up, 4, 0))
    t_cur, t_ahead, t_behind = turned(cur), turned(ahead), turned(behind)
    t_up, t_down = turned(up), turned(down)
    depth = {
        1: jnp.where(low, t_cur, t_ahead) + jnp.where(low, t_behind, t_cur),
        2: ahead + behind,
        3: jnp.where(low, t_ahead, t_down) + jnp.where(low, t_up, t_behind),
        4: up + down,
    }
    total = (3.0 * WEIGHTS[0]) * cur
    for k in range(1, 5):
        near = depth[k]
        near = near + jnp.where(line < 64 - k, pltpu.roll(cur, 128 - k, 1), 0.0)
        near = near + jnp.where(line >= k, pltpu.roll(cur, k, 1), 0.0)
        if k < 4:
            near = near + jnp.where(cell < 4 - k, pltpu.roll(cur, 8 - k, 0), pltpu.roll(right, 4 - k, 0))
            near = near + jnp.where(cell >= k, pltpu.roll(cur, k, 0), pltpu.roll(left, 4 + k, 0))
        else:
            near = near + right + left
        total = total + WEIGHTS[k] * near
    return total


def kernel(
    snap_hbm, refl_hbm, cour_hbm, lags_ref, owners_ref, out_ref,
    snap_v, refl_v, cour_v, load_sem,
    snap_t, snap_r, snap_ss, snap_rs,
    refl_t, refl_r, refl_ss, refl_rs, own_sem,
    lag_v, lag_r, lag_s, lag_ss, lag_rs, lag_sem,
    pick_s, pick_r, pick_ss, pick_rs,
    back_s, back_r, back_ss, back_rs,
    acc_z, acc_zss, acc_zrs,
    acc, acc_ss, acc_rs,
    sum_s, sum_r, sum_ss, sum_rs,
    wave_s, wave_r, wave_ss, wave_rs,
    last_z, last_zss, last_zrs,
    last, last_ss, last_rs,
):
    off = lax.axis_index("off")
    dep = lax.axis_index("dep")
    z, xy = rem(off, 4), div(off, 4)
    y, x = div(xy, 4), rem(xy, 4)
    block = block_of(xy)
    quarter = quarter_of(block, z)
    piece = 4 * block + quarter

    loads = [
        pltpu.make_async_copy(snap_hbm, snap_v, load_sem.at[0]),
        pltpu.make_async_copy(refl_hbm, refl_v, load_sem.at[1]),
        pltpu.make_async_copy(cour_hbm, cour_v, load_sem.at[2]),
    ]
    for load in loads:
        load.start()

    def column_ahead(k):
        return rem(y + div(k, 4), 4) * 4 + rem(x + rem(k, 4), 4)

    def column_behind(k):
        return rem(y + 4 - div(k, 4), 4) * 4 + rem(x + 4 - rem(k, 4), 4)

    def in_plane(column):
        return {"off": column * 4 + z, "dep": dep}

    def in_column(z_to):
        return {"off": xy * 4 + z_to, "dep": dep}

    left, right = device_of(rem(piece + 63, 64)), device_of(rem(piece + 1, 64))
    up, down = rem(dep + 7, 8), rem(dep + 1, 8)
    sides = [
        {"off": right, "dep": dep},
        {"off": left, "dep": dep},
        {"off": off, "dep": down},
        {"off": off, "dep": up},
    ]
    inside = [
        jnp.where(piece > 0, 1.0, 0.0).astype(F32),
        jnp.where(piece < 63, 1.0, 0.0).astype(F32),
        jnp.where(dep > 0, 1.0, 0.0).astype(F32),
        jnp.where(dep < 7, 1.0, 0.0).astype(F32),
    ]

    def remote(src, dst, send, recv, to):
        return pltpu.make_async_remote_copy(
            src_ref=src, dst_ref=dst, send_sem=send, recv_sem=recv, device_id=to, device_id_type=MESH
        )

    def each(lower, upper, body):
        def run(i, carry):
            body(i)
            return carry

        lax.fori_loop(lower, upper, run, 0)

    barrier = pltpu.get_barrier_semaphore()

    def greet(to):
        pl.semaphore_signal(barrier, inc=1, device_id=to, device_id_type=MESH)

    each(1, 16, lambda k: greet(in_plane(column_ahead(k))))
    for k in range(1, 4):
        greet(in_column(rem(z + k, 4)))
    greet(sides[2])
    greet(sides[3])

    lane = lax.broadcasted_iota(jnp.int32, (8, 128), 1)
    lag_row = jnp.zeros((8, 128), jnp.int32)
    for h in range(OFFSETS):
        lag_row = jnp.where(lane == h, lags_ref[h], lag_row)
    lag_v[...] = lag_row
    lag_r[pl.ds(xy, 1)] = lag_row[None]

    identity = jnp.where(
        lax.broadcasted_iota(jnp.int32, (256, 256), 0) == lax.broadcasted_iota(jnp.int32, (256, 256), 1), 1.0, 0.0
    ).astype(BF16)

    loads[0].wait()
    flipped = transposed(identity, snap_v[...]).astype(BF16)
    snap_t[0] = flipped[:, :128]
    snap_t[1] = flipped[:, 128:]

    pl.semaphore_wait(barrier, 20)

    def slab(column):
        return pl.ds(pl.multiple_of(16 * block_of(column), 16), 16)

    def snap_copy(k, to, slot):
        return remote(snap_t.at[:, slab(to), :], snap_r.at[slot], snap_ss.at[k], snap_rs.at[k], in_plane(to))

    def lag_copy(k, to, slot):
        return remote(lag_v, lag_r.at[slot], lag_ss.at[k], lag_rs.at[k], in_plane(to))

    def refl_copy(part, k, to, slot):
        return remote(
            refl_t.at[pl.ds(part * PART, PART), :, slab(to), :],
            refl_r.at[slot, pl.ds(part * PART, PART)],
            refl_ss.at[part, k],
            refl_rs.at[part, k],
            in_plane(to),
        )

    each(1, 16, lambda k: snap_copy(k, column_ahead(k), xy).start())
    snap_r[pl.ds(xy, 1)] = snap_t[:, slab(xy), :][None]

    loads[1].wait()

    def flip_one(h):
        image = transposed(identity, refl_v[h]).astype(BF16)
        refl_t[h, 0] = image[:, :128]
        refl_t[h, 1] = image[:, 128:]

    for part in range(CHUNKS):
        each(part * PART, (part + 1) * PART, flip_one)
        each(1, 16, lambda k: refl_copy(part, k, column_ahead(k), xy).start())
    each(1, 16, lambda k: lag_copy(k, column_ahead(k), xy).start())
    own = pltpu.make_async_copy(refl_t.at[:, :, slab(xy), :], refl_r.at[xy], own_sem)
    own.start()

    loads[2].wait()
    piece_row = lax.broadcasted_iota(jnp.int32, (8, 256), 0)
    piece_col = lax.broadcasted_iota(jnp.int32, (8, 256), 1)
    courant = jnp.zeros((8, 128), F32)
    for half in range(2):
        chosen = jnp.where(
            (piece_col == 4 * piece + piece_row - 4 * half) & (div(piece_row, 4) == half), 1.0, 0.0
        ).astype(BF16)
        rest = cour_v[pl.ds(128 * half, 128), :]
        for _ in range(3):
            head = rest.astype(BF16)
            rest = rest - head.astype(F32)
            courant = courant + transposed(chosen, head)

    each(1, 16, lambda k: snap_copy(k, xy, column_behind(k)).wait_recv())
    quarters = [[] for _ in range(4)]
    for t in range(ITERS):
        owner = owners_ref[t]
        kept = jnp.where(rem(owner, 4) == z, 1.0, 0.0).astype(F32)
        field = snap_r[div(owner, 4)].astype(F32) * kept
        for q in range(4):
            quarters[q].append(field[0, 4 * q : 4 * q + 4])
            quarters[q].append(field[1, 4 * q : 4 * q + 4])
    for q in range(4):
        pick_s[q] = jnp.concatenate(quarters[q], axis=0).astype(BF16)

    def pick_copy(k):
        z_to = rem(z + k, 4)
        return remote(
            pick_s.at[quarter_of(block, z_to)], pick_r.at[k - 1], pick_ss.at[k - 1], pick_rs.at[k - 1], in_column(z_to)
        )

    for k in range(1, 4):
        pick_copy(k).start()
    back = pick_s[quarter].astype(F32)
    for k in range(1, 4):
        pick_copy(k).wait_recv()
        back = back + pick_r[k - 1].astype(F32)
    back_s[...] = back.astype(BF16)

    def back_copy(side):
        return remote(back_s, back_r.at[side], back_ss.at[side], back_rs.at[side], sides[side])

    for side in range(4):
        back_copy(side).start()
    for side in range(4):
        back_copy(side).wait_recv()

    def accelerate(pair):
        rows = pl.ds(pl.multiple_of(16 * pair, 16), 16)
        cur = back_s[rows, :].astype(F32)
        rim = [back_r[side, rows, :].astype(F32) * inside[side] for side in range(4)]
        for half in range(2):
            part = slice(8 * half, 8 * half + 8)
            value = courant * laplace(cur[part], *[v[part] for v in rim])
            acc_z[quarter, 2 * pair + half] = value

    each(0, ITERS // 2, accelerate)

    def acc_zcopy(k, slot):
        return remote(acc_z.at[slot], acc_z.at[slot], acc_zss.at[k - 1], acc_zrs.at[k - 1], in_column(rem(z + k, 4)))

    for k in range(1, 4):
        acc_zcopy(k, quarter).start()
    for k in range(1, 4):
        acc_zcopy(k, quarter_of(block, rem(z + 4 - k, 4))).wait_recv()

    def gather_acc(t):
        parts = [acc_z[q, t] for q in range(4)]
        for half in range(2):
            acc[t, half, 32:48, :] = jnp.concatenate([v[4 * half : 4 * half + 4] for v in parts], axis=0)

    each(0, ITERS, gather_acc)

    def acc_copy(i, step):
        to = column_of(rem(block + 16 + step, 16))
        return remote(
            acc.at[:, :, 32:48, :], acc.at[:, :, 16 * (2 - step) : 16 * (2 - step) + 16, :],
            acc_ss.at[i], acc_rs.at[i], in_plane(to),
        )

    steps = (1, -1, 2, -2)
    for i, step in enumerate(steps):
        acc_copy(i, step).start()
    own.wait()
    each(1, 16, lambda k: lag_copy(k, xy, column_behind(k)).wait_recv())
    lag_copy_s = pltpu.make_async_copy(lag_r, lag_s, lag_sem)
    lag_copy_s.start()
    lag_copy_s.wait()
    for part in range(CHUNKS):
        each(1, 16, lambda k: refl_copy(part, k, xy, column_behind(k)).wait_recv())
    for i, step in enumerate(steps):
        acc_copy(i, step).wait_recv()
    for i, step in enumerate(steps):

        @pl.when((block - step < 0) | (block - step > 15))
        def _():
            def clear(t):
                for half in range(2):
                    acc[t, half, 16 * (2 - step) : 16 * (2 - step) + 16, :] = jnp.zeros((16, 128), F32)

            each(0, ITERS, clear)

    for half in range(2):

        def add_device(s, sums):
            sums = list(sums)
            for h in range(OFFSETS):
                image = refl_r[s, h, half].astype(F32)
                start = LAG - lag_s[s, 0, h]
                for t in range(ITERS):
                    sums[t] = sums[t] + image * acc[t, half, pl.ds(start, 16), :]
            return tuple(sums)

        sums = lax.fori_loop(0, 16, add_device, tuple(jnp.zeros((16, 128), F32) for _ in range(ITERS)))
        for t in range(ITERS):
            for q in range(4):
                sum_s[q, t, 4 * half : 4 * half + 4, :] = sums[t][4 * q : 4 * q + 4]

    def sum_copy(k):
        z_to = rem(z + k, 4)
        return remote(
            sum_s.at[quarter_of(block, z_to)], sum_r.at[k - 1], sum_ss.at[k - 1], sum_rs.at[k - 1], in_column(z_to)
        )

    for k in range(1, 4):
        sum_copy(k).start()
    for k in range(1, 4):
        sum_copy(k).wait_recv()

    def source(t):
        return sum_s[quarter, t] + sum_r[0, t] + sum_r[1, t] + sum_r[2, t]

    def wave_copy(t, side):
        return remote(
            wave_s.at[t], wave_r.at[t, side], wave_ss.at[t, side], wave_rs.at[t, side], sides[side]
        )

    def advance(t, carry):
        cur, previous = carry
        wave_s[t - 1] = cur
        for side in range(4):
            wave_copy(t - 1, side).start()
        ready = 2.0 * cur - previous + source(t)
        for side in range(4):
            wave_copy(t - 1, side).wait_recv()
        rim = [wave_r[t - 1, side] * inside[side] for side in range(4)]
        return ready + courant * laplace(cur, *rim), cur

    wave, _ = lax.fori_loop(1, ITERS, advance, (source(0), jnp.zeros((8, 128), F32)))

    last_z[pl.ds(quarter, 1)] = wave[None]

    def last_zcopy(k, slot):
        return remote(last_z.at[slot], last_z.at[slot], last_zss.at[k - 1], last_zrs.at[k - 1], in_column(rem(z + k, 4)))

    for k in range(1, 4):
        last_zcopy(k, quarter).start()
    for k in range(1, 4):
        last_zcopy(k, quarter_of(block, rem(z + 4 - k, 4))).wait_recv()
    parts = [last_z[q] for q in range(4)]
    for half in range(2):
        last[half, slab(xy), :] = jnp.concatenate([v[4 * half : 4 * half + 4] for v in parts], axis=0)

    def last_copy(k, to, column):
        rows = slab(column)
        return remote(last.at[:, rows, :], last.at[:, rows, :], last_ss.at[k], last_rs.at[k], in_plane(to))

    each(1, 16, lambda k: last_copy(k, column_ahead(k), xy).start())
    each(1, 16, lambda k: last_copy(k, xy, column_behind(k)).wait_recv())
    for half in range(2):
        out_ref[pl.ds(128 * half, 128), :] = last[half].T

    each(1, 16, lambda k: snap_copy(k, column_ahead(k), xy).wait_send())
    each(1, 16, lambda k: lag_copy(k, column_ahead(k), xy).wait_send())
    for part in range(CHUNKS):
        each(1, 16, lambda k: refl_copy(part, k, column_ahead(k), xy).wait_send())
    for k in range(1, 4):
        pick_copy(k).wait_send()
        acc_zcopy(k, quarter).wait_send()
        sum_copy(k).wait_send()
        last_zcopy(k, quarter).wait_send()
    for side in range(4):
        back_copy(side).wait_send()
        each(0, ITERS - 1, lambda t: wave_copy(t, side).wait_send())
    for i, step in enumerate(steps):
        acc_copy(i, step).wait_send()
    each(1, 16, lambda k: last_copy(k, column_ahead(k), xy).wait_send())


def per_device(snapshots, reflect, courant, lags, owners):
    depth, rows, columns = courant.shape
    lines = depth * rows
    dma = pltpu.SemaphoreType.DMA
    any_space = pl.BlockSpec(memory_space=pl.ANY)
    scalars = pl.BlockSpec(memory_space=pltpu.SMEM)
    out = pl.pallas_call(
        kernel,
        out_shape=jax.ShapeDtypeStruct((lines, columns), F32),
        in_specs=[any_space, any_space, any_space, scalars, scalars],
        out_specs=pl.BlockSpec(memory_space=pltpu.VMEM),
        scratch_shapes=[
            pltpu.VMEM((256, 256), BF16), pltpu.VMEM((OFFSETS, 256, 256), BF16), pltpu.VMEM((256, 256), F32), dma((3,)),
            pltpu.VMEM((2, 256, 128), BF16), pltpu.VMEM((16, 2, 16, 128), BF16), dma((16,)), dma((16,)),
            pltpu.VMEM((OFFSETS, 2, 256, 128), BF16), pltpu.VMEM((16, OFFSETS, 2, 16, 128), BF16),
            dma((CHUNKS, 16)), dma((CHUNKS, 16)), dma,
            pltpu.VMEM((8, 128), jnp.int32), pltpu.VMEM((16, 8, 128), jnp.int32), pltpu.SMEM((16, 8, 128), jnp.int32),
            dma((16,)), dma((16,)), dma,
            pltpu.VMEM((4, 64, 128), BF16), pltpu.VMEM((3, 64, 128), BF16), dma((3,)), dma((3,)),
            pltpu.VMEM((64, 128), BF16), pltpu.VMEM((4, 64, 128), BF16), dma((4,)), dma((4,)),
            pltpu.VMEM((4, ITERS, 8, 128), F32), dma((3,)), dma((3,)),
            pltpu.VMEM((ITERS, 2, 80, 128), F32), dma((4,)), dma((4,)),
            pltpu.VMEM((4, ITERS, 8, 128), F32), pltpu.VMEM((3, ITERS, 8, 128), F32), dma((3,)), dma((3,)),
            pltpu.VMEM((ITERS - 1, 8, 128), F32), pltpu.VMEM((ITERS - 1, 4, 8, 128), F32),
            dma((ITERS - 1, 4)), dma((ITERS - 1, 4)),
            pltpu.VMEM((4, 8, 128), F32), dma((3,)), dma((3,)),
            pltpu.VMEM((2, 256, 128), F32), dma((16,)), dma((16,)),
        ],
        compiler_params=pltpu.CompilerParams(
            collective_id=0, has_side_effects=True, vmem_limit_bytes=32 * 1024 * 1024
        ),
        name="born",
    )(
        snapshots.reshape(lines, columns),
        reflect.reshape(reflect.shape[0], lines, columns),
        courant.reshape(lines, columns),
        lags,
        owners,
    )
    return out.reshape(courant.shape)


def solution(mesh):
    in_specs = (
        P("off", "dep", None, None),
        P("off", "dep", None, None),
        P("dep", None, None),
        P("off"),
        P(),
    )
    return jax.shard_map(
        per_device, mesh=mesh, in_specs=in_specs, out_specs=P("dep", None, None), check_vma=False
    )
```

```python
import jax
import jax.numpy as jnp
from jax import lax
from jax.experimental import pallas as pl
from jax.experimental.pallas import tpu as pltpu
from jax.sharding import PartitionSpec as P

ITERS = 8
LAG = 32
WEIGHTS = (-205.0 / 72.0, 8.0 / 5.0, -1.0 / 5.0, 8.0 / 315.0, -1.0 / 560.0)
MESH = pl.DeviceIdType.MESH
F32 = jnp.float32
BF16 = jnp.bfloat16
OFFSETS = 12
CHUNKS = 3
PART = OFFSETS // CHUNKS
FIRST = 3
STAR = ((-1, 0), (1, 0), (0, -1), (0, 1))
FAR = ((-2, 0), (2, 0), (0, -2), (0, 2), (-1, -1), (-1, 1), (1, -1), (1, 1))
NEAR = STAR + FAR
ROUNDS = 4


def rem(a, n):
    return lax.rem(a, jnp.int32(n))


def div(a, n):
    return lax.div(a, jnp.int32(n))


def snake(i):
    y, x = div(i, 4), rem(i, 4)
    return 4 * y + x + rem(y, 2) * (3 - 2 * x)


def laplace(cur, prev, nxt, up, down):
    row = lax.broadcasted_iota(jnp.int32, (8, 128), 0)
    line = rem(row, 4)
    halves = lambda v: (v[:8], v[8:])
    turned = lambda v: pltpu.roll(v, 4, 0)
    (u0, u1), (c0, c1), (d0, d1) = halves(up), halves(cur), halves(down)
    tu0, tu1, tc0, tc1, td0, td1 = [turned(v) for v in (u0, u1, c0, c1, d0, d1)]
    join = lambda a, b: jnp.where(row < 4, a, b)
    uu, uc, cc, cd, dd = join(tu0, tu1), join(tu1, tc0), join(tc0, tc1), join(tc1, td0), join(td0, td1)
    depth = (
        {1: cc + uc, 2: c1 + u1, 3: cd + uu, 4: d0 + u0},
        {1: cd + cc, 2: d0 + c0, 3: dd + uc, 4: d1 + u1},
    )
    out = []
    for half in range(2):
        c, p, n = halves(cur)[half], halves(prev)[half], halves(nxt)[half]
        total = (3.0 * WEIGHTS[0]) * c
        for k in range(1, 5):
            near = depth[half][k] + pltpu.roll(c, 128 - k, 1) + pltpu.roll(c, k, 1)
            if k < 4:
                near = near + jnp.where(line < 4 - k, pltpu.roll(c, 8 - k, 0), pltpu.roll(n, 4 - k, 0))
                near = near + jnp.where(line >= k, pltpu.roll(c, k, 0), pltpu.roll(p, 4 + k, 0))
            else:
                near = near + n + p
            total = total + WEIGHTS[k] * near
        out.append(total)
    return jnp.concatenate(out, axis=0)


def windows(field):
    first, second = field[:, :128], field[:, 128:]
    lane = lax.broadcasted_iota(jnp.int32, first.shape, 1)
    f32, s32 = pltpu.roll(first, 32, 1), pltpu.roll(second, 32, 1)
    f96, s96 = pltpu.roll(first, 96, 1), pltpu.roll(second, 96, 1)
    return (
        jnp.where(lane < 32, 0.0, f32),
        jnp.where(lane < 96, f96, s96),
        jnp.where(lane < 32, f32, s32),
        jnp.where(lane < 96, s96, 0.0),
    )


def packed(top, bottom):
    lane = lax.broadcasted_iota(jnp.int32, top.shape, 1)
    return jnp.where(lane < 64, pltpu.roll(top, 96, 1), pltpu.roll(bottom, 32, 1))


def unpacked(a, b):
    lane = lax.broadcasted_iota(jnp.int32, a.shape, 1)
    return jnp.where(lane < 64, a, pltpu.roll(b, 64, 1)), jnp.where(lane < 64, pltpu.roll(a, 64, 1), b)


def kernel(
    snap_hbm, refl_hbm, cour_hbm, lags_ref, owners_ref, out_ref,
    snap_v, refl_v, cour_v, load_sem,
    snap_t, snap_r, snap_ss, snap_rs,
    refl_t, refl_r, refl_ss, refl_rs, own_sem,
    lag_v, lag_r, lag_s, lag_ss, lag_rs, lag_sem,
    cour_w, cour_s, cour_r, cour_ss, cour_rs,
    pick_s, pick_r, pick_ss, pick_rs,
    back_s, back_r, back_ss, back_rs,
    acc_w, acc_z, acc_zss, acc_zrs, moved,
    sum_s, sum_r, sum_ss, sum_rs,
    wave_s, wave_r, wave_f, wave_ss, wave_rs,
    last_z, last_zss, last_zrs,
    last, last_ss, last_rs,
):
    off = lax.axis_index("off")
    dep = lax.axis_index("dep")
    z, xy = rem(off, 4), div(off, 4)
    y, x = div(xy, 4), rem(xy, 4)
    block = snake(xy)

    loads = [
        pltpu.make_async_copy(snap_hbm, snap_v, load_sem.at[0]),
        pltpu.make_async_copy(refl_hbm, refl_v, load_sem.at[1]),
        pltpu.make_async_copy(cour_hbm, cour_v, load_sem.at[2]),
    ]
    for load in loads:
        load.start()

    def column_ahead(k):
        return rem(y + div(k, 4), 4) * 4 + rem(x + rem(k, 4), 4)

    def column_behind(k):
        return rem(y + 4 - div(k, 4), 4) * 4 + rem(x + 4 - rem(k, 4), 4)

    def in_plane(column):
        return {"off": column * 4 + z, "dep": dep}

    def in_column(z_to):
        return {"off": xy * 4 + z_to, "dep": dep}

    def beside(place):
        rows, layers = place
        return {"off": snake(rem(block + 16 + rows, 16)) * 4 + z, "dep": rem(dep + 8 + layers, 8)}

    def inside(place):
        b, d = block + place[0], dep + place[1]
        return jnp.where((b >= 0) & (b < 16) & (d >= 0) & (d < 8), 1.0, 0.0).astype(F32)

    def against(place):
        return (-place[0], -place[1])

    def remote(src, dst, send, recv, to):
        return pltpu.make_async_remote_copy(
            src_ref=src, dst_ref=dst, send_sem=send, recv_sem=recv, device_id=to, device_id_type=MESH
        )

    def each(lower, upper, body):
        def run(i, carry):
            body(i)
            return carry

        lax.fori_loop(lower, upper, run, 0)

    barrier = pltpu.get_barrier_semaphore()

    def greet(to):
        pl.semaphore_signal(barrier, inc=1, device_id=to, device_id_type=MESH)

    each(1, 16, lambda k: greet(in_plane(column_ahead(k))))
    for k in range(1, 4):
        greet(in_column(rem(z + k, 4)))
    met = [place for place in NEAR if place[1] != 0]
    for place in met:
        greet(beside(place))

    lane = lax.broadcasted_iota(jnp.int32, (8, 128), 1)
    lag_row = jnp.zeros((8, 128), jnp.int32)
    for h in range(OFFSETS):
        lag_row = jnp.where(lane == h, lags_ref[h], lag_row)
    lag_v[...] = lag_row
    lag_r[pl.ds(xy, 1)] = lag_row[None]

    to_row = lax.broadcasted_iota(jnp.int32, (256, 256), 0)
    from_row = lax.broadcasted_iota(jnp.int32, (256, 256), 1)
    wanted = rem(div(to_row, 4), 4) * 64 + div(to_row, 16) * 4 + rem(to_row, 4)
    order = jnp.where(from_row == wanted, 1.0, 0.0).astype(BF16)

    def ordered(image):
        return jnp.dot(order, image, preferred_element_type=F32).astype(BF16).reshape(16, 16, 256)

    loads[0].wait()
    snap_t[...] = ordered(snap_v[...])

    pl.semaphore_wait(barrier, 18 + len(met))
    def snap_copy(k, to, slot):
        return remote(snap_t.at[snake(to)], snap_r.at[slot], snap_ss.at[k], snap_rs.at[k], in_plane(to))

    def lag_copy(k, to, slot):
        return remote(lag_v, lag_r.at[slot], lag_ss.at[k], lag_rs.at[k], in_plane(to))

    def refl_copy(part, k, to, slot):
        return remote(
            refl_t.at[snake(to), pl.ds(part * PART, PART)],
            refl_r.at[slot, pl.ds(part * PART, PART)],
            refl_ss.at[part, k],
            refl_rs.at[part, k],
            in_plane(to),
        )

    each(1, 16, lambda k: snap_copy(k, column_ahead(k), xy).start())
    snap_r[pl.ds(xy, 1)] = snap_t[pl.ds(block, 1)]
    loads[1].wait()

    def order_one(h):
        refl_t[:, pl.ds(h, 1)] = ordered(refl_v[h])[:, None]

    for part in range(CHUNKS):
        each(part * PART, (part + 1) * PART, order_one)
        each(1, 16, lambda k: refl_copy(part, k, column_ahead(k), xy).start())
    each(1, 16, lambda k: lag_copy(k, column_ahead(k), xy).start())
    own = pltpu.make_async_copy(refl_t.at[block], refl_r.at[xy], own_sem)
    own.start()
    loads[2].wait()
    odd = rem(block, 2)
    layers = []
    for layer in range(4):
        rows = cour_v[layer, pl.ds(pl.multiple_of(8 * div(block, 2), 8), 8), :]
        layers.append(jnp.where(odd == 0, rows[:4], rows[4:]))
    for q, window in enumerate(windows(jnp.concatenate(layers, axis=0))):
        cour_w[q] = window
    courant = cour_w[z]
    cour_s[...] = courant

    def cour_copy(i):
        return remote(cour_s, cour_r.at[i], cour_ss.at[i], cour_rs.at[i], beside(against(STAR[i])))

    for i in range(4):
        cour_copy(i).start()
    each(1, 16, lambda k: snap_copy(k, xy, column_behind(k)).wait_recv())
    for t in range(ITERS):
        owner = owners_ref[t]
        kept = jnp.where(rem(owner, 4) == z, 1.0, 0.0).astype(F32)
        field = snap_r[div(owner, 4)].astype(F32) * kept
        for q, window in enumerate(windows(field)):
            pick_s[q, 16 * t : 16 * t + 16, :] = window.astype(BF16)

    def pick_copy(k):
        z_to = rem(z + k, 4)
        return remote(pick_s.at[z_to], pick_r.at[k - 1], pick_ss.at[k - 1], pick_rs.at[k - 1], in_column(z_to))

    for k in range(1, 4):
        pick_copy(k).start()
    back = pick_s[z].astype(F32)
    for k in range(1, 4):
        pick_copy(k).wait_recv()
        back = back + pick_r[k - 1].astype(F32)
    back_s[...] = back.astype(BF16)
    def back_copy(i):
        return remote(back_s, back_r.at[i], back_ss.at[i], back_rs.at[i], beside(against(STAR[i])))

    for i in range(4):
        back_copy(i).start()
    for i in range(4):
        back_copy(i).wait_recv()

    def accelerate(t):
        rows = pl.ds(pl.multiple_of(16 * t, 16), 16)
        rim = [back_r[i, rows, :].astype(F32) * inside(STAR[i]) for i in range(4)]
        acc_w[rows, :] = courant * laplace(back_s[rows, :].astype(F32), *rim)

    each(0, ITERS, accelerate)
    acc_z[pl.ds(z, 1)] = packed(acc_w[:64, :], acc_w[64:, :])[None]
    def acc_zcopy(k, slot):
        return remote(acc_z.at[slot], acc_z.at[slot], acc_zss.at[k - 1], acc_zrs.at[k - 1], in_column(rem(z + k, 4)))

    for k in range(1, 4):
        acc_zcopy(k, z).start()
    for k in range(1, 4):
        acc_zcopy(k, rem(z + 4 - k, 4)).wait_recv()
    wide = lax.broadcasted_iota(jnp.int32, (64, 128), 1)
    for side in range(2):
        a = unpacked(acc_z[0], acc_z[1])[side]
        b = unpacked(acc_z[2], acc_z[3])[side]
        rows = slice(64 * side, 64 * side + 64)

        def move_right(lag):
            ra, rb = pltpu.roll(a, lag, 1), pltpu.roll(b, lag, 1)
            moved[LAG + lag, rows, :128] = jnp.where(wide < lag, 0.0, ra)
            moved[LAG + lag, rows, 128:] = jnp.where(wide < lag, ra, rb)

        def move_left(lag):
            ra, rb = pltpu.roll(a, 128 - lag, 1), pltpu.roll(b, 128 - lag, 1)
            moved[LAG - lag, rows, :128] = jnp.where(wide < 128 - lag, ra, rb)
            moved[LAG - lag, rows, 128:] = jnp.where(wide < 128 - lag, rb, 0.0)

        each(0, LAG + 1, move_right)
        each(1, LAG + 1, move_left)
    own.wait()
    each(1, 16, lambda k: lag_copy(k, xy, column_behind(k)).wait_recv())
    scalars = pltpu.make_async_copy(lag_r, lag_s, lag_sem)
    scalars.start()
    scalars.wait()
    sums = tuple(jnp.zeros((16, 256), F32) for _ in range(ITERS))
    for part in range(CHUNKS):
        each(1, 16, lambda k: refl_copy(part, k, xy, column_behind(k)).wait_recv())

        def add_device(s, sums):
            sums = list(sums)
            for h in range(part * PART, (part + 1) * PART):
                image = refl_r[s, h].astype(F32)
                place = lag_s[s, 0, h] + LAG
                for t in range(ITERS):
                    sums[t] = sums[t] + image * moved[place, 16 * t : 16 * t + 16, :]
            return tuple(sums)

        sums = lax.fori_loop(0, 16, add_device, sums)
    for t in range(ITERS):
        for q, window in enumerate(windows(sums[t])):
            sum_s[q, 16 * t : 16 * t + 16, :] = window
    spans = ((0, 16 * FIRST), (16 * FIRST, 16 * (ITERS - FIRST)))

    def sum_copy(i, k):
        z_to = rem(z + k, 4)
        rows = pl.ds(*spans[i])
        return remote(
            sum_s.at[z_to, rows, :], sum_r.at[k - 1, rows, :], sum_ss.at[i, k - 1], sum_rs.at[i, k - 1], in_column(z_to)
        )

    for i in range(2):
        for k in range(1, 4):
            sum_copy(i, k).start()
    for k in range(1, 4):
        sum_copy(0, k).wait_recv()

    def source(t):
        rows = slice(16 * t, 16 * t + 16)
        return sum_s[z, rows, :] + sum_r[0, rows, :] + sum_r[1, rows, :] + sum_r[2, rows, :]

    for i in range(4):
        cour_copy(i).wait_recv()

    def wave_copy(r, i):
        to = beside(against(NEAR[i]))
        if i < 4:
            return remote(wave_s.at[r], wave_r.at[r, i], wave_ss.at[r, i], wave_rs.at[r, i], to)
        return remote(wave_s.at[r, 0], wave_f.at[r, i - 4], wave_ss.at[r, i], wave_rs.at[r, i], to)

    def sent(r):
        return range(len(NEAR) if r < ROUNDS - 1 else 4)

    def at(a, b):
        return (a[0] + b[0], a[1] + b[1])

    old = {place: jnp.zeros((16, 128), F32) for place in ((0, 0),) + STAR}
    wave = source(0)
    masks = {place: inside(place) for place in NEAR}
    courants = {(0, 0): courant}
    for i, place in enumerate(STAR):
        courants[place] = cour_r[i]
    for r in range(ROUNDS):
        wave_s[r, 0] = wave
        if r == 1:
            for k in range(1, 4):
                sum_copy(1, k).wait_recv()
        now = source(2 * r + 1)
        if r < ROUNDS - 1:
            wave_s[r, 1] = now
        for i in sent(r):
            wave_copy(r, i).start()
        field = {(0, 0): wave}
        for i in sent(r):
            wave_copy(r, i).wait_recv()
            place = NEAR[i]
            field[place] = (wave_r[r, i, 0] if i < 4 else wave_f[r, i - 4]) * masks[place]
        ahead = {}
        for place in ((0, 0),) + (STAR if r < ROUNDS - 1 else ()):
            rim = [field[at(place, side)] for side in STAR]
            term = now if place == (0, 0) else wave_r[r, STAR.index(place), 1]
            value = 2.0 * field[place] - old[place] + courants[place] * laplace(field[place], *rim) + term
            ahead[place] = value if place == (0, 0) else value * masks[place]
        if r == ROUNDS - 1:
            wave = ahead[(0, 0)]
            break
        rim = [ahead[side] for side in STAR]
        wave = 2.0 * ahead[(0, 0)] - wave + courant * laplace(ahead[(0, 0)], *rim) + source(2 * r + 2)
        old = ahead
    last_z[pl.ds(z, 1)] = packed(wave[:8], wave[8:])[None]

    def last_zcopy(k, slot):
        return remote(last_z.at[slot], last_z.at[slot], last_zss.at[k - 1], last_zrs.at[k - 1], in_column(rem(z + k, 4)))

    for k in range(1, 4):
        last_zcopy(k, z).start()
    for k in range(1, 4):
        last_zcopy(k, rem(z + 4 - k, 4)).wait_recv()
    west, east = unpacked(last_z[0], last_z[1]), unpacked(last_z[2], last_z[3])
    slab = jnp.concatenate([jnp.concatenate([west[i], east[i]], axis=1) for i in range(2)], axis=0)
    last[pl.ds(block, 1)] = slab[None]

    def last_copy(k, to, column):
        place = snake(column)
        return remote(last.at[place], last.at[place], last_ss.at[k], last_rs.at[k], in_plane(to))

    each(1, 16, lambda k: last_copy(k, column_ahead(k), xy).start())
    each(1, 16, lambda k: last_copy(k, xy, column_behind(k)).wait_recv())
    for layer in range(4):
        for pair in range(8):
            out_ref[layer, 8 * pair : 8 * pair + 8, :] = jnp.concatenate(
                [last[2 * pair + i, 4 * layer : 4 * layer + 4, :] for i in range(2)], axis=0
            )
    each(1, 16, lambda k: snap_copy(k, column_ahead(k), xy).wait_send())
    each(1, 16, lambda k: lag_copy(k, column_ahead(k), xy).wait_send())
    for part in range(CHUNKS):
        each(1, 16, lambda k: refl_copy(part, k, column_ahead(k), xy).wait_send())
    for k in range(1, 4):
        pick_copy(k).wait_send()
        acc_zcopy(k, z).wait_send()
        sum_copy(0, k).wait_send()
        sum_copy(1, k).wait_send()
        last_zcopy(k, z).wait_send()
    for i in range(4):
        back_copy(i).wait_send()
        cour_copy(i).wait_send()
    for r in range(ROUNDS):
        for i in sent(r):
            wave_copy(r, i).wait_send()
    each(1, 16, lambda k: last_copy(k, column_ahead(k), xy).wait_send())


def per_device(snapshots, reflect, courant, lags, owners):
    depth, rows, columns = courant.shape
    lines = depth * rows
    dma = pltpu.SemaphoreType.DMA
    any_space = pl.BlockSpec(memory_space=pl.ANY)
    scalars = pl.BlockSpec(memory_space=pltpu.SMEM)
    return pl.pallas_call(
        kernel,
        out_shape=jax.ShapeDtypeStruct(courant.shape, F32),
        in_specs=[any_space, any_space, any_space, scalars, scalars],
        out_specs=pl.BlockSpec(memory_space=pltpu.VMEM),
        scratch_shapes=[
            pltpu.VMEM((256, 256), BF16), pltpu.VMEM((OFFSETS, 256, 256), BF16), pltpu.VMEM((4, 64, 256), F32), dma((3,)),
            pltpu.VMEM((16, 16, 256), BF16), pltpu.VMEM((16, 16, 256), BF16), dma((16,)), dma((16,)),
            pltpu.VMEM((16, OFFSETS, 16, 256), BF16), pltpu.VMEM((16, OFFSETS, 16, 256), BF16),
            dma((CHUNKS, 16)), dma((CHUNKS, 16)), dma,
            pltpu.VMEM((8, 128), jnp.int32), pltpu.VMEM((16, 8, 128), jnp.int32), pltpu.SMEM((16, 8, 128), jnp.int32),
            dma((16,)), dma((16,)), dma,
            pltpu.VMEM((4, 16, 128), F32), pltpu.VMEM((16, 128), F32), pltpu.VMEM((4, 16, 128), F32), dma((4,)), dma((4,)),
            pltpu.VMEM((4, 128, 128), BF16), pltpu.VMEM((3, 128, 128), BF16), dma((3,)), dma((3,)),
            pltpu.VMEM((128, 128), BF16), pltpu.VMEM((4, 128, 128), BF16), dma((4,)), dma((4,)),
            pltpu.VMEM((128, 128), F32), pltpu.VMEM((4, 64, 128), F32), dma((3,)), dma((3,)),
            pltpu.VMEM((2 * LAG + 1, 128, 256), F32),
            pltpu.VMEM((4, 128, 128), F32), pltpu.VMEM((3, 128, 128), F32), dma((2, 3)), dma((2, 3)),
            pltpu.VMEM((ROUNDS, 2, 16, 128), F32), pltpu.VMEM((ROUNDS, 4, 2, 16, 128), F32),
            pltpu.VMEM((ROUNDS - 1, len(FAR), 16, 128), F32), dma((ROUNDS, len(NEAR))), dma((ROUNDS, len(NEAR))),
            pltpu.VMEM((4, 8, 128), F32), dma((3,)), dma((3,)),
            pltpu.VMEM((16, 16, 256), F32), dma((16,)), dma((16,)),
        ],
        compiler_params=pltpu.CompilerParams(
            collective_id=0, has_side_effects=True, vmem_limit_bytes=60 * 1024 * 1024
        ),
        name="born",
    )(
        snapshots.reshape(lines, columns),
        reflect.reshape(reflect.shape[0], lines, columns),
        courant,
        lags,
        owners,
    )


def solution(mesh):
    in_specs = (
        P("off", "dep", None, None),
        P("off", "dep", None, None),
        P("dep", None, None),
        P("off"),
        P(),
    )
    return jax.shard_map(
        per_device, mesh=mesh, in_specs=in_specs, out_specs=P("dep", None, None), check_vma=False
    )
```

```python
import jax
import jax.numpy as jnp
from jax import lax
from jax.experimental import pallas as pl
from jax.experimental.pallas import tpu as pltpu
from jax.sharding import PartitionSpec as P

ITERS = 8
LAG = 32
WEIGHTS = (-205.0 / 72.0, 8.0 / 5.0, -1.0 / 5.0, 8.0 / 315.0, -1.0 / 560.0)
MESH = pl.DeviceIdType.MESH
F32 = jnp.float32
BF16 = jnp.bfloat16
OFFSETS = 12
CHUNKS = 3
PART = OFFSETS // CHUNKS
FIRST = 2
STAR = ((-1, 0), (1, 0), (0, -1), (0, 1))
FAR = ((-2, 0), (2, 0), (0, -2), (0, 2), (-1, -1), (-1, 1), (1, -1), (1, 1))
NEAR = STAR + FAR
ROUNDS = 4


def rem(a, n):
    return lax.rem(a, jnp.int32(n))


def div(a, n):
    return lax.div(a, jnp.int32(n))


def snake(i):
    y, x = div(i, 4), rem(i, 4)
    return 4 * y + x + rem(y, 2) * (3 - 2 * x)


def inner(cur):
    row = lax.broadcasted_iota(jnp.int32, (8, 128), 0)
    line = rem(row, 4)
    c0, c1 = cur[:8], cur[8:]
    t0, t1 = pltpu.roll(c0, 4, 0), pltpu.roll(c1, 4, 0)
    both = jnp.where(row < 4, t0, t1)
    depth = (
        {1: both + jnp.where(row < 4, 0.0, t0), 2: c1, 3: jnp.where(row < 4, t1, 0.0)},
        {1: both + jnp.where(row < 4, t1, 0.0), 2: c0, 3: jnp.where(row < 4, 0.0, t0)},
    )
    out = []
    for half, c in enumerate((c0, c1)):
        total = (3.0 * WEIGHTS[0]) * c
        for k in range(1, 5):
            near = pltpu.roll(c, 128 - k, 1) + pltpu.roll(c, k, 1)
            if k < 4:
                near = near + depth[half][k]
                near = near + jnp.where(line < 4 - k, pltpu.roll(c, 8 - k, 0), 0.0)
                near = near + jnp.where(line >= k, pltpu.roll(c, k, 0), 0.0)
            total = total + WEIGHTS[k] * near
        out.append(total)
    return jnp.concatenate(out, axis=0)


def rim(side, tile):
    row = lax.broadcasted_iota(jnp.int32, (8, 128), 0)
    line = rem(row, 4)
    w = WEIGHTS
    a, b = tile[:8], tile[8:]
    if side[1] == 0:
        out = []
        for v in (a, b):
            total = w[4] * v
            for k in range(1, 4):
                if side[0] > 0:
                    total = total + w[k] * jnp.where(line < 4 - k, 0.0, pltpu.roll(v, 4 - k, 0))
                else:
                    total = total + w[k] * jnp.where(line < k, pltpu.roll(v, 4 + k, 0), 0.0)
            out.append(total)
        return jnp.concatenate(out, axis=0)
    ta, tb = pltpu.roll(a, 4, 0), pltpu.roll(b, 4, 0)
    both = jnp.where(row < 4, ta, tb)
    if side[1] > 0:
        last = jnp.where(row < 4, 0.0, ta)
        return jnp.concatenate(
            [w[3] * last + w[4] * a, w[1] * last + w[2] * a + w[3] * both + w[4] * b], axis=0
        )
    first = jnp.where(row < 4, tb, 0.0)
    return jnp.concatenate(
        [w[1] * first + w[2] * b + w[3] * both + w[4] * a, w[3] * first + w[4] * b], axis=0
    )


def windows(field):
    first, second = field[:, :128], field[:, 128:]
    lane = lax.broadcasted_iota(jnp.int32, first.shape, 1)
    f32, s32 = pltpu.roll(first, 32, 1), pltpu.roll(second, 32, 1)
    f96, s96 = pltpu.roll(first, 96, 1), pltpu.roll(second, 96, 1)
    return (
        jnp.where(lane < 32, 0.0, f32),
        jnp.where(lane < 96, f96, s96),
        jnp.where(lane < 32, f32, s32),
        jnp.where(lane < 96, s96, 0.0),
    )


def packed(top, bottom):
    lane = lax.broadcasted_iota(jnp.int32, top.shape, 1)
    return jnp.where(lane < 64, pltpu.roll(top, 96, 1), pltpu.roll(bottom, 32, 1))


def unpacked(a, b):
    lane = lax.broadcasted_iota(jnp.int32, a.shape, 1)
    return jnp.where(lane < 64, a, pltpu.roll(b, 64, 1)), jnp.where(lane < 64, pltpu.roll(a, 64, 1), b)


def kernel(
    snap_hbm, refl_hbm, cour_hbm, lags_ref, owners_ref, out_ref,
    snap_v, refl_v, cour_v, load_sem,
    snap_t, snap_r, snap_ss, snap_rs,
    refl_t, refl_r, refl_ss, refl_rs, own_sem,
    lag_v, lag_r, lag_s, lag_ss, lag_rs, lag_sem,
    cour_w, cour_s, cour_r, cour_ss, cour_rs,
    pick_s, pick_r, pick_ss, pick_rs,
    back_s, back_r, back_ss, back_rs,
    acc_w, acc_z, acc_zss, acc_zrs, moved,
    sum_s, sum_r, sum_ss, sum_rs,
    wave_s, wave_r, wave_f, wave_ss, wave_rs,
    last_z, last_zss, last_zrs,
    last, last_ss, last_rs,
):
    off = lax.axis_index("off")
    dep = lax.axis_index("dep")
    z, xy = rem(off, 4), div(off, 4)
    y, x = div(xy, 4), rem(xy, 4)
    block = snake(xy)

    loads = [
        pltpu.make_async_copy(snap_hbm, snap_v, load_sem.at[0]),
        pltpu.make_async_copy(refl_hbm, refl_v, load_sem.at[1]),
        pltpu.make_async_copy(cour_hbm, cour_v, load_sem.at[2]),
    ]
    for load in loads:
        load.start()

    def column_ahead(k):
        return rem(y + div(k, 4), 4) * 4 + rem(x + rem(k, 4), 4)

    def column_behind(k):
        return rem(y + 4 - div(k, 4), 4) * 4 + rem(x + 4 - rem(k, 4), 4)

    def in_plane(column):
        return {"off": column * 4 + z, "dep": dep}

    def in_column(z_to):
        return {"off": xy * 4 + z_to, "dep": dep}

    def beside(place):
        rows, layers = place
        return {"off": snake(rem(block + 16 + rows, 16)) * 4 + z, "dep": rem(dep + 8 + layers, 8)}

    def inside(place):
        b, d = block + place[0], dep + place[1]
        return jnp.where((b >= 0) & (b < 16) & (d >= 0) & (d < 8), 1.0, 0.0).astype(F32)

    def against(place):
        return (-place[0], -place[1])

    def remote(src, dst, send, recv, to):
        return pltpu.make_async_remote_copy(
            src_ref=src, dst_ref=dst, send_sem=send, recv_sem=recv, device_id=to, device_id_type=MESH
        )

    def each(lower, upper, body):
        def run(i, carry):
            body(i)
            return carry

        lax.fori_loop(lower, upper, run, 0)

    masks = {place: inside(place) for place in NEAR}
    barrier = pltpu.get_barrier_semaphore()

    def greet(to):
        pl.semaphore_signal(barrier, inc=1, device_id=to, device_id_type=MESH)

    each(1, 16, lambda k: greet(in_plane(column_ahead(k))))
    for k in range(1, 4):
        greet(in_column(rem(z + k, 4)))
    met = [place for place in NEAR if place[1] != 0]
    for place in met:
        greet(beside(place))

    lane = lax.broadcasted_iota(jnp.int32, (8, 128), 1)
    lag_row = jnp.zeros((8, 128), jnp.int32)
    for h in range(OFFSETS):
        lag_row = jnp.where(lane == h, lags_ref[h], lag_row)
    lag_v[...] = lag_row
    lag_r[pl.ds(xy, 1)] = lag_row[None]

    to_row = lax.broadcasted_iota(jnp.int32, (256, 256), 0)
    from_row = lax.broadcasted_iota(jnp.int32, (256, 256), 1)
    wanted = rem(div(to_row, 4), 4) * 64 + div(to_row, 16) * 4 + rem(to_row, 4)
    order = jnp.where(from_row == wanted, 1.0, 0.0).astype(BF16)

    def ordered(image):
        return jnp.dot(order, image, preferred_element_type=F32).astype(BF16).reshape(16, 16, 256)

    loads[0].wait()
    snap_t[...] = ordered(snap_v[...])

    loads[1].wait()

    def order_one(h):
        refl_t[:, pl.ds(h, 1)] = ordered(refl_v[h])[:, None]

    each(0, PART, order_one)

    pl.semaphore_wait(barrier, 18 + len(met))
    def snap_copy(k, to, slot):
        return remote(snap_t.at[snake(to)], snap_r.at[slot], snap_ss.at[k], snap_rs.at[k], in_plane(to))

    def lag_copy(k, to, slot):
        return remote(lag_v, lag_r.at[slot], lag_ss.at[k], lag_rs.at[k], in_plane(to))

    def refl_copy(part, k, to, slot):
        return remote(
            refl_t.at[snake(to), pl.ds(part * PART, PART)],
            refl_r.at[slot, pl.ds(part * PART, PART)],
            refl_ss.at[part, k],
            refl_rs.at[part, k],
            in_plane(to),
        )

    each(1, 16, lambda k: snap_copy(k, column_ahead(k), xy).start())
    snap_r[pl.ds(xy, 1)] = snap_t[pl.ds(block, 1)]
    for part in range(CHUNKS):
        if part:
            each(part * PART, (part + 1) * PART, order_one)
        each(1, 16, lambda k: refl_copy(part, k, column_ahead(k), xy).start())
    each(1, 16, lambda k: lag_copy(k, column_ahead(k), xy).start())
    own = pltpu.make_async_copy(refl_t.at[block], refl_r.at[xy], own_sem)
    own.start()
    loads[2].wait()
    odd = rem(block, 2)
    layers = []
    for layer in range(4):
        rows = cour_v[layer, pl.ds(pl.multiple_of(8 * div(block, 2), 8), 8), :]
        layers.append(jnp.where(odd == 0, rows[:4], rows[4:]))
    for q, window in enumerate(windows(jnp.concatenate(layers, axis=0))):
        cour_w[q] = window
    courant = cour_w[z]
    cour_s[...] = courant

    def cour_copy(i):
        return remote(cour_s, cour_r.at[i], cour_ss.at[i], cour_rs.at[i], beside(against(STAR[i])))

    for i in range(4):
        cour_copy(i).start()
    each(1, 16, lambda k: snap_copy(k, xy, column_behind(k)).wait_recv())
    for t in range(ITERS):
        owner = owners_ref[t]
        kept = jnp.where(rem(owner, 4) == z, 1.0, 0.0).astype(F32)
        field = snap_r[div(owner, 4)].astype(F32) * kept
        for q, window in enumerate(windows(field)):
            pick_s[q, 16 * t : 16 * t + 16, :] = window.astype(BF16)

    def pick_copy(k):
        z_to = rem(z + k, 4)
        return remote(pick_s.at[z_to], pick_r.at[k - 1], pick_ss.at[k - 1], pick_rs.at[k - 1], in_column(z_to))

    for k in range(1, 4):
        pick_copy(k).start()
    back = pick_s[z].astype(F32)
    for k in range(1, 4):
        pick_copy(k).wait_recv()
        back = back + pick_r[k - 1].astype(F32)
    back_s[...] = back.astype(BF16)
    def back_copy(i):
        return remote(back_s, back_r.at[i], back_ss.at[i], back_rs.at[i], beside(against(STAR[i])))

    for i in reversed(range(4)):
        back_copy(i).start()
    for i in range(4):
        back_copy(i).wait_recv()

    def accelerate(i):
        for j in range(4):
            rows = pl.ds(pl.multiple_of(64 * i + 16 * j, 16), 16)
            total = inner(back_s[rows, :].astype(F32))
            for n, side in enumerate(STAR):
                total = total + rim(side, back_r[n, rows, :].astype(F32)) * masks[side]
            acc_w[rows, :] = courant * total

    each(0, ITERS // 4, accelerate)
    acc_z[pl.ds(z, 1)] = packed(acc_w[:64, :], acc_w[64:, :])[None]
    def acc_zcopy(k, slot):
        return remote(acc_z.at[slot], acc_z.at[slot], acc_zss.at[k - 1], acc_zrs.at[k - 1], in_column(rem(z + k, 4)))

    for k in range(1, 4):
        acc_zcopy(k, z).start()
    for k in range(1, 4):
        acc_zcopy(k, rem(z + 4 - k, 4)).wait_recv()
    first = jnp.concatenate(unpacked(acc_z[0], acc_z[1]), axis=0)
    second = jnp.concatenate(unpacked(acc_z[2], acc_z[3]), axis=0)

    def move_all(rows, unrolled):
        a, b = first[rows], second[rows]
        wide = lax.broadcasted_iota(jnp.int32, a.shape, 1)
        moved[LAG, rows, :128] = a
        moved[LAG, rows, 128:] = b

        def move(i):
            for j in range(1, unrolled + 1):
                lag = unrolled * i + j
                ra, rb = pltpu.roll(a, lag, 1), pltpu.roll(b, lag, 1)
                moved[LAG + lag, rows, :128] = jnp.where(wide < lag, 0.0, ra)
                moved[LAG + lag, rows, 128:] = jnp.where(wide < lag, ra, rb)
                rest = 128 - lag
                ra, rb = pltpu.roll(a, rest, 1), pltpu.roll(b, rest, 1)
                moved[LAG - lag, rows, :128] = jnp.where(wide < rest, ra, rb)
                moved[LAG - lag, rows, 128:] = jnp.where(wide < rest, rb, 0.0)

        each(0, LAG // unrolled, move)

    def add_parts(steps, ready):
        sums = tuple(jnp.zeros((16, 256), F32) for _ in steps)
        for part in range(CHUNKS):
            ready(part)

            def add_device(s, sums):
                sums = list(sums)
                for h in range(part * PART, (part + 1) * PART):
                    image = refl_r[s, h].astype(F32)
                    place = lag_s[s, 0, h] + LAG
                    for i, t in enumerate(steps):
                        sums[i] = sums[i] + image * moved[place, 16 * t : 16 * t + 16, :]
                return tuple(sums)

            sums = lax.fori_loop(0, 16, add_device, sums)
        for i, t in enumerate(steps):
            for q, window in enumerate(windows(sums[i])):
                sum_s[q, 16 * t : 16 * t + 16, :] = window

    def arrive(part):
        each(1, 16, lambda k: refl_copy(part, k, xy, column_behind(k)).wait_recv())

    own.wait()
    each(1, 16, lambda k: lag_copy(k, xy, column_behind(k)).wait_recv())
    scalars = pltpu.make_async_copy(lag_r, lag_s, lag_sem)
    scalars.start()
    scalars.wait()
    move_all(slice(0, 16 * FIRST), 8)
    add_parts(range(FIRST), arrive)
    spans = ((0, 16 * FIRST), (16 * FIRST, 16 * (ITERS - FIRST)))

    def sum_copy(i, k):
        z_to = rem(z + k, 4)
        rows = pl.ds(*spans[i])
        return remote(
            sum_s.at[z_to, rows, :], sum_r.at[k - 1, rows, :], sum_ss.at[i, k - 1], sum_rs.at[i, k - 1], in_column(z_to)
        )

    for k in range(1, 4):
        sum_copy(0, k).start()
    move_all(slice(16 * FIRST, 16 * ITERS), 4)
    add_parts(range(FIRST, ITERS), lambda part: None)
    for k in range(1, 4):
        sum_copy(1, k).start()

    each(1, 16, lambda k: snap_copy(k, column_ahead(k), xy).wait_send())
    each(1, 16, lambda k: lag_copy(k, column_ahead(k), xy).wait_send())
    for part in range(CHUNKS):
        each(1, 16, lambda k: refl_copy(part, k, column_ahead(k), xy).wait_send())
    for k in range(1, 4):
        pick_copy(k).wait_send()
        acc_zcopy(k, z).wait_send()
    for i in range(4):
        back_copy(i).wait_send()
        cour_copy(i).wait_send()
    for k in range(1, 4):
        sum_copy(0, k).wait_recv()

    def source(t):
        rows = slice(16 * t, 16 * t + 16)
        return sum_s[z, rows, :] + sum_r[0, rows, :] + sum_r[1, rows, :] + sum_r[2, rows, :]

    for i in range(4):
        cour_copy(i).wait_recv()

    def wave_copy(r, i):
        to = beside(against(NEAR[i]))
        if i < 4:
            return remote(wave_s.at[r], wave_r.at[r, i], wave_ss.at[r, i], wave_rs.at[r, i], to)
        return remote(wave_s.at[r, 0], wave_f.at[r, i - 4], wave_ss.at[r, i], wave_rs.at[r, i], to)

    def sent(r):
        return range(len(NEAR) if r < ROUNDS - 1 else 4)

    def at(a, b):
        return (a[0] + b[0], a[1] + b[1])

    here = (0, 0)
    old = {place: jnp.zeros((16, 128), F32) for place in (here,) + STAR}
    wave = source(0)
    courants = {here: courant}
    for i, place in enumerate(STAR):
        courants[place] = cour_r[i] * masks[place]
    for r in range(ROUNDS):
        more = r < ROUNDS - 1
        wave_s[r, 0] = wave
        now = source(2 * r + 1)
        if more:
            wave_s[r, 1] = now
        for i in reversed(sent(r)):
            wave_copy(r, i).start()
        if r:
            for i in sent(r - 1):
                wave_copy(r - 1, i).wait_send()
        slope = {here: inner(wave)}
        base = {here: 2.0 * wave - old[here] + now}
        if more:
            for side in STAR:
                slope[side] = rim(against(side), wave)
        for i in (0, 1, 4, 5, 2, 3, 6, 7, 8, 9, 10, 11):
            if i not in sent(r):
                continue
            wave_copy(r, i).wait_recv()
            place = NEAR[i]
            tile = (wave_r[r, i, 0] if i < 4 else wave_f[r, i - 4]) * masks[place]
            for side in STAR:
                to = at(place, against(side))
                if to in slope and (to != place) and (more or to == here):
                    slope[to] = slope[to] + rim(side, tile)
            if i < 4 and more:
                slope[place] = slope[place] + inner(tile)
                base[place] = 2.0 * tile - old[place] + wave_r[r, i, 1] * masks[place]
        ahead = {place: base[place] + courants[place] * slope[place] for place in base}
        if not more:
            wave = ahead[here]
            break
        if r == 0:
            for k in range(1, 4):
                sum_copy(1, k).wait_recv()
        total = inner(ahead[here])
        for side in STAR:
            total = total + rim(side, ahead[side])
        wave = 2.0 * ahead[here] - wave + courant * total + source(2 * r + 2)
        old = ahead
    last_z[pl.ds(z, 1)] = packed(wave[:8], wave[8:])[None]

    def last_zcopy(k, slot):
        return remote(last_z.at[slot], last_z.at[slot], last_zss.at[k - 1], last_zrs.at[k - 1], in_column(rem(z + k, 4)))

    for k in range(1, 4):
        last_zcopy(k, z).start()
    for k in range(1, 4):
        last_zcopy(k, rem(z + 4 - k, 4)).wait_recv()
    west, east = unpacked(last_z[0], last_z[1]), unpacked(last_z[2], last_z[3])
    slab = jnp.concatenate([jnp.concatenate([west[i], east[i]], axis=1) for i in range(2)], axis=0)
    last[pl.ds(block, 1)] = slab[None]

    def last_copy(k, to, column):
        place = snake(column)
        return remote(last.at[place], last.at[place], last_ss.at[k], last_rs.at[k], in_plane(to))

    each(1, 16, lambda k: last_copy(k, column_ahead(k), xy).start())
    each(1, 16, lambda k: last_copy(k, xy, column_behind(k)).wait_recv())
    for layer in range(4):
        for pair in range(8):
            out_ref[layer, 8 * pair : 8 * pair + 8, :] = jnp.concatenate(
                [last[2 * pair + i, 4 * layer : 4 * layer + 4, :] for i in range(2)], axis=0
            )
    for k in range(1, 4):
        sum_copy(0, k).wait_send()
        sum_copy(1, k).wait_send()
        last_zcopy(k, z).wait_send()
    for i in sent(ROUNDS - 1):
        wave_copy(ROUNDS - 1, i).wait_send()
    each(1, 16, lambda k: last_copy(k, column_ahead(k), xy).wait_send())


def per_device(snapshots, reflect, courant, lags, owners):
    depth, rows, columns = courant.shape
    lines = depth * rows
    dma = pltpu.SemaphoreType.DMA
    any_space = pl.BlockSpec(memory_space=pl.ANY)
    scalars = pl.BlockSpec(memory_space=pltpu.SMEM)
    return pl.pallas_call(
        kernel,
        out_shape=jax.ShapeDtypeStruct(courant.shape, F32),
        in_specs=[any_space, any_space, any_space, scalars, scalars],
        out_specs=pl.BlockSpec(memory_space=pltpu.VMEM),
        scratch_shapes=[
            pltpu.VMEM((256, 256), BF16), pltpu.VMEM((OFFSETS, 256, 256), BF16), pltpu.VMEM((4, 64, 256), F32), dma((3,)),
            pltpu.VMEM((16, 16, 256), BF16), pltpu.VMEM((16, 16, 256), BF16), dma((16,)), dma((16,)),
            pltpu.VMEM((16, OFFSETS, 16, 256), BF16), pltpu.VMEM((16, OFFSETS, 16, 256), BF16),
            dma((CHUNKS, 16)), dma((CHUNKS, 16)), dma,
            pltpu.VMEM((8, 128), jnp.int32), pltpu.VMEM((16, 8, 128), jnp.int32), pltpu.SMEM((16, 8, 128), jnp.int32),
            dma((16,)), dma((16,)), dma,
            pltpu.VMEM((4, 16, 128), F32), pltpu.VMEM((16, 128), F32), pltpu.VMEM((4, 16, 128), F32), dma((4,)), dma((4,)),
            pltpu.VMEM((4, 128, 128), BF16), pltpu.VMEM((3, 128, 128), BF16), dma((3,)), dma((3,)),
            pltpu.VMEM((128, 128), BF16), pltpu.VMEM((4, 128, 128), BF16), dma((4,)), dma((4,)),
            pltpu.VMEM((128, 128), F32), pltpu.VMEM((4, 64, 128), F32), dma((3,)), dma((3,)),
            pltpu.VMEM((2 * LAG + 1, 128, 256), F32),
            pltpu.VMEM((4, 128, 128), F32), pltpu.VMEM((3, 128, 128), F32), dma((2, 3)), dma((2, 3)),
            pltpu.VMEM((ROUNDS, 2, 16, 128), F32), pltpu.VMEM((ROUNDS, 4, 2, 16, 128), F32),
            pltpu.VMEM((ROUNDS - 1, len(FAR), 16, 128), F32), dma((ROUNDS, len(NEAR))), dma((ROUNDS, len(NEAR))),
            pltpu.VMEM((4, 8, 128), F32), dma((3,)), dma((3,)),
            pltpu.VMEM((16, 16, 256), F32), dma((16,)), dma((16,)),
        ],
        compiler_params=pltpu.CompilerParams(
            collective_id=0, has_side_effects=True, vmem_limit_bytes=60 * 1024 * 1024
        ),
        name="born",
    )(
        snapshots.reshape(lines, columns),
        reflect.reshape(reflect.shape[0], lines, columns),
        courant,
        lags,
        owners,
    )


def solution(mesh):
    in_specs = (
        P("off", "dep", None, None),
        P("off", "dep", None, None),
        P("dep", None, None),
        P("off"),
        P(),
    )
    return jax.shard_map(
        per_device, mesh=mesh, in_specs=in_specs, out_specs=P("dep", None, None), check_vma=False
    )
```

```python
import jax
import jax.numpy as jnp
from jax import lax
from jax.experimental import pallas as pl
from jax.experimental.pallas import tpu as pltpu
from jax.sharding import PartitionSpec as P

ITERS = 8
LAG = 32
WEIGHTS = (-205.0 / 72.0, 8.0 / 5.0, -1.0 / 5.0, 8.0 / 315.0, -1.0 / 560.0)
MESH = pl.DeviceIdType.MESH
F32 = jnp.float32
BF16 = jnp.bfloat16
OFFSETS = 12
CHUNKS = 3
PART = OFFSETS // CHUNKS
FIRST = 2
STAR = ((-1, 0), (1, 0), (0, -1), (0, 1))
FAR = ((-2, 0), (2, 0), (0, -2), (0, 2), (-1, -1), (-1, 1), (1, -1), (1, 1))
NEAR = STAR + FAR
ROUNDS = 4


def rem(a, n):
    return lax.rem(a, jnp.int32(n))


def div(a, n):
    return lax.div(a, jnp.int32(n))


def snake(i):
    y, x = div(i, 4), rem(i, 4)
    return 4 * y + x + rem(y, 2) * (3 - 2 * x)


def inner(cur):
    row = lax.broadcasted_iota(jnp.int32, (8, 128), 0)
    line = rem(row, 4)
    c0, c1 = cur[:8], cur[8:]
    t0, t1 = pltpu.roll(c0, 4, 0), pltpu.roll(c1, 4, 0)
    both = jnp.where(row < 4, t0, t1)
    depth = (
        {1: both + jnp.where(row < 4, 0.0, t0), 2: c1, 3: jnp.where(row < 4, t1, 0.0)},
        {1: both + jnp.where(row < 4, t1, 0.0), 2: c0, 3: jnp.where(row < 4, 0.0, t0)},
    )
    out = []
    for half, c in enumerate((c0, c1)):
        total = (3.0 * WEIGHTS[0]) * c
        for k in range(1, 5):
            near = pltpu.roll(c, 128 - k, 1) + pltpu.roll(c, k, 1)
            if k < 4:
                near = near + depth[half][k]
                near = near + jnp.where(line < 4 - k, pltpu.roll(c, 8 - k, 0), 0.0)
                near = near + jnp.where(line >= k, pltpu.roll(c, k, 0), 0.0)
            total = total + WEIGHTS[k] * near
        out.append(total)
    return jnp.concatenate(out, axis=0)


def rim(side, tile):
    row = lax.broadcasted_iota(jnp.int32, (8, 128), 0)
    line = rem(row, 4)
    w = WEIGHTS
    a, b = tile[:8], tile[8:]
    if side[1] == 0:
        out = []
        for v in (a, b):
            total = w[4] * v
            for k in range(1, 4):
                if side[0] > 0:
                    total = total + w[k] * jnp.where(line < 4 - k, 0.0, pltpu.roll(v, 4 - k, 0))
                else:
                    total = total + w[k] * jnp.where(line < k, pltpu.roll(v, 4 + k, 0), 0.0)
            out.append(total)
        return jnp.concatenate(out, axis=0)
    ta, tb = pltpu.roll(a, 4, 0), pltpu.roll(b, 4, 0)
    both = jnp.where(row < 4, ta, tb)
    if side[1] > 0:
        last = jnp.where(row < 4, 0.0, ta)
        return jnp.concatenate(
            [w[3] * last + w[4] * a, w[1] * last + w[2] * a + w[3] * both + w[4] * b], axis=0
        )
    first = jnp.where(row < 4, tb, 0.0)
    return jnp.concatenate(
        [w[1] * first + w[2] * b + w[3] * both + w[4] * a, w[3] * first + w[4] * b], axis=0
    )


def windows(field):
    first, second = field[:, :128], field[:, 128:]
    lane = lax.broadcasted_iota(jnp.int32, first.shape, 1)
    f32, s32 = pltpu.roll(first, 32, 1), pltpu.roll(second, 32, 1)
    f96, s96 = pltpu.roll(first, 96, 1), pltpu.roll(second, 96, 1)
    return (
        jnp.where(lane < 32, 0.0, f32),
        jnp.where(lane < 96, f96, s96),
        jnp.where(lane < 32, f32, s32),
        jnp.where(lane < 96, s96, 0.0),
    )


def packed(top, bottom):
    lane = lax.broadcasted_iota(jnp.int32, top.shape, 1)
    return jnp.where(lane < 64, pltpu.roll(top, 96, 1), pltpu.roll(bottom, 32, 1))


def unpacked(a, b):
    lane = lax.broadcasted_iota(jnp.int32, a.shape, 1)
    return jnp.where(lane < 64, a, pltpu.roll(b, 64, 1)), jnp.where(lane < 64, pltpu.roll(a, 64, 1), b)


def kernel(
    snap_hbm, refl_hbm, cour_hbm, lags_ref, owners_ref, out_ref,
    snap_v, refl_v, cour_v, load_sem,
    snap_t, snap_r, snap_ss, snap_rs,
    refl_t, refl_r, refl_ss, refl_rs, own_sem,
    lag_v, lag_r, lag_s, lag_ss, lag_rs, lag_sem,
    cour_w, cour_s, cour_r, cour_ss, cour_rs,
    pick_s, pick_r, pick_ss, pick_rs,
    back_s, back_r, back_ss, back_rs,
    acc_w, acc_z, acc_zss, acc_zrs, moved,
    sum_s, sum_r, sum_ss, sum_rs,
    wave_s, wave_r, wave_f, wave_ss, wave_rs,
    last_z, last_zss, last_zrs,
    last, last_ss, last_rs,
):
    off = lax.axis_index("off")
    dep = lax.axis_index("dep")
    z, xy = rem(off, 4), div(off, 4)
    y, x = div(xy, 4), rem(xy, 4)
    block = snake(xy)

    loads = [
        pltpu.make_async_copy(snap_hbm, snap_v, load_sem.at[0]),
        pltpu.make_async_copy(refl_hbm, refl_v, load_sem.at[1]),
        pltpu.make_async_copy(cour_hbm, cour_v, load_sem.at[2]),
    ]
    for load in loads:
        load.start()

    def column_ahead(k):
        return rem(y + div(k, 4), 4) * 4 + rem(x + rem(k, 4), 4)

    def column_behind(k):
        return rem(y + 4 - div(k, 4), 4) * 4 + rem(x + 4 - rem(k, 4), 4)

    def in_plane(column):
        return {"off": column * 4 + z, "dep": dep}

    def in_column(z_to):
        return {"off": xy * 4 + z_to, "dep": dep}

    def beside(place):
        rows, layers = place
        return {"off": snake(rem(block + 16 + rows, 16)) * 4 + z, "dep": rem(dep + 8 + layers, 8)}

    def inside(place):
        b, d = block + place[0], dep + place[1]
        return jnp.where((b >= 0) & (b < 16) & (d >= 0) & (d < 8), 1.0, 0.0).astype(F32)

    def against(place):
        return (-place[0], -place[1])

    def remote(src, dst, send, recv, to):
        return pltpu.make_async_remote_copy(
            src_ref=src, dst_ref=dst, send_sem=send, recv_sem=recv, device_id=to, device_id_type=MESH
        )

    def each(lower, upper, body):
        def run(i, carry):
            body(i)
            return carry

        lax.fori_loop(lower, upper, run, 0)

    def every(body):
        for k in range(1, 16):
            body(jnp.int32(k))

    masks = {place: inside(place) for place in NEAR}
    barrier = pltpu.get_barrier_semaphore()

    def greet(to):
        pl.semaphore_signal(barrier, inc=1, device_id=to, device_id_type=MESH)

    every(lambda k: greet(in_plane(column_ahead(k))))
    for k in range(1, 4):
        greet(in_column(rem(z + k, 4)))
    met = [place for place in NEAR if place[1] != 0]
    for place in met:
        greet(beside(place))

    lane = lax.broadcasted_iota(jnp.int32, (8, 128), 1)
    lag_row = jnp.zeros((8, 128), jnp.int32)
    for h in range(OFFSETS):
        lag_row = jnp.where(lane == h, lags_ref[h], lag_row)
    lag_v[...] = lag_row
    lag_r[pl.ds(xy, 1)] = lag_row[None]

    to_row = lax.broadcasted_iota(jnp.int32, (256, 256), 0)
    from_row = lax.broadcasted_iota(jnp.int32, (256, 256), 1)
    wanted = rem(div(to_row, 4), 4) * 64 + div(to_row, 16) * 4 + rem(to_row, 4)
    order = jnp.where(from_row == wanted, 1.0, 0.0).astype(BF16)

    def ordered(image):
        return jnp.dot(order, image, preferred_element_type=F32).astype(BF16).reshape(16, 16, 256)

    loads[0].wait()
    snap_t[...] = ordered(snap_v[...])

    loads[1].wait()

    def order_one(h):
        refl_t[:, pl.ds(h, 1)] = ordered(refl_v[h])[:, None]

    each(0, PART, order_one)

    pl.semaphore_wait(barrier, 18 + len(met))
    def snap_copy(k, to, slot):
        return remote(snap_t.at[snake(to)], snap_r.at[slot], snap_ss.at[k], snap_rs.at[k], in_plane(to))

    def lag_copy(k, to, slot):
        return remote(lag_v, lag_r.at[slot], lag_ss.at[k], lag_rs.at[k], in_plane(to))

    def refl_copy(part, k, to, slot):
        return remote(
            refl_t.at[snake(to), pl.ds(part * PART, PART)],
            refl_r.at[slot, pl.ds(part * PART, PART)],
            refl_ss.at[part, k],
            refl_rs.at[part, k],
            in_plane(to),
        )

    every(lambda k: snap_copy(k, column_ahead(k), xy).start())
    snap_r[pl.ds(xy, 1)] = snap_t[pl.ds(block, 1)]
    def send_part(part):
        if part:
            each(part * PART, (part + 1) * PART, order_one)
        every(lambda k: refl_copy(part, k, column_ahead(k), xy).start())

    for part in (0, 1):
        send_part(part)
    every(lambda k: lag_copy(k, column_ahead(k), xy).start())
    loads[2].wait()
    odd = rem(block, 2)
    layers = []
    for layer in range(4):
        rows = cour_v[layer, pl.ds(pl.multiple_of(8 * div(block, 2), 8), 8), :]
        layers.append(jnp.where(odd == 0, rows[:4], rows[4:]))
    for q, window in enumerate(windows(jnp.concatenate(layers, axis=0))):
        cour_w[q] = window
    courant = cour_w[z]
    cour_s[...] = courant

    def cour_copy(i):
        return remote(cour_s, cour_r.at[i], cour_ss.at[i], cour_rs.at[i], beside(against(STAR[i])))

    for i in range(4):
        cour_copy(i).start()
    every(lambda k: snap_copy(k, xy, column_behind(k)).wait_recv())
    for t in range(ITERS):
        owner = owners_ref[t]
        kept = jnp.where(rem(owner, 4) == z, 1.0, 0.0).astype(F32)
        field = snap_r[div(owner, 4)].astype(F32) * kept
        for q, window in enumerate(windows(field)):
            pick_s[q, 16 * t : 16 * t + 16, :] = window.astype(BF16)

    def pick_copy(k):
        z_to = rem(z + k, 4)
        return remote(pick_s.at[z_to], pick_r.at[k - 1], pick_ss.at[k - 1], pick_rs.at[k - 1], in_column(z_to))

    for k in range(1, 4):
        pick_copy(k).start()
    back = pick_s[z].astype(F32)
    for k in range(1, 4):
        pick_copy(k).wait_recv()
        back = back + pick_r[k - 1].astype(F32)
    back_s[...] = back.astype(BF16)
    def back_copy(i):
        return remote(back_s, back_r.at[i], back_ss.at[i], back_rs.at[i], beside(against(STAR[i])))

    for i in reversed(range(4)):
        back_copy(i).start()
    send_part(2)
    own = pltpu.make_async_copy(refl_t.at[block], refl_r.at[xy], own_sem)
    own.start()
    for i in range(4):
        back_copy(i).wait_recv()

    def accelerate(i):
        for j in range(4):
            rows = pl.ds(pl.multiple_of(64 * i + 16 * j, 16), 16)
            total = inner(back_s[rows, :].astype(F32))
            for n, side in enumerate(STAR):
                total = total + rim(side, back_r[n, rows, :].astype(F32)) * masks[side]
            acc_w[rows, :] = courant * total

    each(0, ITERS // 4, accelerate)
    acc_z[pl.ds(z, 1)] = packed(acc_w[:64, :], acc_w[64:, :])[None]
    def acc_zcopy(k, slot):
        return remote(acc_z.at[slot], acc_z.at[slot], acc_zss.at[k - 1], acc_zrs.at[k - 1], in_column(rem(z + k, 4)))

    for k in range(1, 4):
        acc_zcopy(k, z).start()
    for k in range(1, 4):
        acc_zcopy(k, rem(z + 4 - k, 4)).wait_recv()
    first = jnp.concatenate(unpacked(acc_z[0], acc_z[1]), axis=0)
    second = jnp.concatenate(unpacked(acc_z[2], acc_z[3]), axis=0)

    def move_all(rows, unrolled):
        a, b = first[rows], second[rows]
        wide = lax.broadcasted_iota(jnp.int32, a.shape, 1)
        moved[LAG, rows, :128] = a
        moved[LAG, rows, 128:] = b

        def move(i):
            for j in range(1, unrolled + 1):
                lag = unrolled * i + j
                ra, rb = pltpu.roll(a, lag, 1), pltpu.roll(b, lag, 1)
                moved[LAG + lag, rows, :128] = jnp.where(wide < lag, 0.0, ra)
                moved[LAG + lag, rows, 128:] = jnp.where(wide < lag, ra, rb)
                rest = 128 - lag
                ra, rb = pltpu.roll(a, rest, 1), pltpu.roll(b, rest, 1)
                moved[LAG - lag, rows, :128] = jnp.where(wide < rest, ra, rb)
                moved[LAG - lag, rows, 128:] = jnp.where(wide < rest, rb, 0.0)

        each(0, LAG // unrolled, move)

    def add_parts(steps, ready):
        sums = tuple(jnp.zeros((16, 256), F32) for _ in steps)
        for part in range(CHUNKS):
            ready(part)

            def add_device(s, sums):
                sums = list(sums)
                for h in range(part * PART, (part + 1) * PART):
                    image = refl_r[s, h].astype(F32)
                    place = lag_s[s, 0, h] + LAG
                    for i, t in enumerate(steps):
                        sums[i] = sums[i] + image * moved[place, 16 * t : 16 * t + 16, :]
                return tuple(sums)

            sums = lax.fori_loop(0, 16, add_device, sums)
        for i, t in enumerate(steps):
            for q, window in enumerate(windows(sums[i])):
                sum_s[q, 16 * t : 16 * t + 16, :] = window

    def arrive(part):
        every(lambda k: refl_copy(part, k, xy, column_behind(k)).wait_recv())

    own.wait()
    every(lambda k: lag_copy(k, xy, column_behind(k)).wait_recv())
    scalars = pltpu.make_async_copy(lag_r, lag_s, lag_sem)
    scalars.start()
    scalars.wait()
    move_all(slice(0, 16 * FIRST), 8)
    add_parts(range(FIRST), arrive)
    spans = ((0, FIRST), (FIRST, 1), (FIRST + 1, 2), (FIRST + 3, 2), (FIRST + 5, 1))

    def sum_copy(i, k):
        z_to = rem(z + k, 4)
        rows = pl.ds(16 * spans[i][0], 16 * spans[i][1])
        return remote(
            sum_s.at[z_to, rows, :], sum_r.at[k - 1, rows, :], sum_ss.at[i, k - 1], sum_rs.at[i, k - 1], in_column(z_to)
        )

    for k in range(1, 4):
        sum_copy(0, k).start()
    move_all(slice(16 * FIRST, 16 * ITERS), 4)
    add_parts(range(FIRST, ITERS), lambda part: None)
    for k in range(1, 4):
        sum_copy(1, k).start()

    every(lambda k: snap_copy(k, column_ahead(k), xy).wait_send())
    every(lambda k: lag_copy(k, column_ahead(k), xy).wait_send())
    for part in range(CHUNKS):
        every(lambda k: refl_copy(part, k, column_ahead(k), xy).wait_send())
    for k in range(1, 4):
        pick_copy(k).wait_send()
        acc_zcopy(k, z).wait_send()
    for i in range(4):
        back_copy(i).wait_send()
        cour_copy(i).wait_send()
    for k in range(1, 4):
        sum_copy(0, k).wait_recv()

    def source(t):
        rows = slice(16 * t, 16 * t + 16)
        return sum_s[z, rows, :] + sum_r[0, rows, :] + sum_r[1, rows, :] + sum_r[2, rows, :]

    for i in range(4):
        cour_copy(i).wait_recv()

    def wave_copy(r, i):
        to = beside(against(NEAR[i]))
        if i < 4:
            return remote(wave_s.at[r], wave_r.at[r, i], wave_ss.at[r, i], wave_rs.at[r, i], to)
        return remote(wave_s.at[r, 0], wave_f.at[r, i - 4], wave_ss.at[r, i], wave_rs.at[r, i], to)

    def sent(r):
        return range(len(NEAR) if r < ROUNDS - 1 else 4)

    def at(a, b):
        return (a[0] + b[0], a[1] + b[1])

    here = (0, 0)
    old = {place: jnp.zeros((16, 128), F32) for place in (here,) + STAR}
    wave = source(0)
    courants = {here: courant}
    for i, place in enumerate(STAR):
        courants[place] = cour_r[i] * masks[place]
    for r in range(ROUNDS):
        more = r < ROUNDS - 1
        wave_s[r, 0] = wave
        now = source(2 * r + 1)
        if more:
            wave_s[r, 1] = now
        for i in reversed(sent(r)):
            wave_copy(r, i).start()
        if more:
            for k in range(1, 4):
                sum_copy(2 + r, k).start()
        if r:
            for i in sent(r - 1):
                wave_copy(r - 1, i).wait_send()
        slope = {here: inner(wave)}
        base = {here: 2.0 * wave - old[here] + now}
        if more:
            for side in STAR:
                slope[side] = rim(against(side), wave)
        for i in (0, 1, 4, 5, 2, 3, 6, 7, 8, 9, 10, 11):
            if i not in sent(r):
                continue
            wave_copy(r, i).wait_recv()
            place = NEAR[i]
            tile = (wave_r[r, i, 0] if i < 4 else wave_f[r, i - 4]) * masks[place]
            for side in STAR:
                to = at(place, against(side))
                if to in slope and (to != place) and (more or to == here):
                    slope[to] = slope[to] + rim(side, tile)
            if i < 4 and more:
                slope[place] = slope[place] + inner(tile)
                base[place] = 2.0 * tile - old[place] + wave_r[r, i, 1] * masks[place]
        ahead = {place: base[place] + courants[place] * slope[place] for place in base}
        if not more:
            wave = ahead[here]
            break
        for i in (1, 2) if r == 0 else (2 + r,):
            for k in range(1, 4):
                sum_copy(i, k).wait_recv()
        total = inner(ahead[here])
        for side in STAR:
            total = total + rim(side, ahead[side])
        wave = 2.0 * ahead[here] - wave + courant * total + source(2 * r + 2)
        old = ahead
    last_z[pl.ds(z, 1)] = packed(wave[:8], wave[8:])[None]

    def last_zcopy(k, slot):
        return remote(last_z.at[slot], last_z.at[slot], last_zss.at[k - 1], last_zrs.at[k - 1], in_column(rem(z + k, 4)))

    for k in range(1, 4):
        last_zcopy(k, z).start()
    for k in range(1, 4):
        last_zcopy(k, rem(z + 4 - k, 4)).wait_recv()
    west, east = unpacked(last_z[0], last_z[1]), unpacked(last_z[2], last_z[3])
    slab = jnp.concatenate([jnp.concatenate([west[i], east[i]], axis=1) for i in range(2)], axis=0)
    last[pl.ds(block, 1)] = slab[None]

    def last_copy(k, to, column):
        place = snake(column)
        return remote(last.at[place], last.at[place], last_ss.at[k], last_rs.at[k], in_plane(to))

    every(lambda k: last_copy(k, column_ahead(k), xy).start())
    every(lambda k: last_copy(k, xy, column_behind(k)).wait_recv())
    for layer in range(4):
        for pair in range(8):
            out_ref[layer, 8 * pair : 8 * pair + 8, :] = jnp.concatenate(
                [last[2 * pair + i, 4 * layer : 4 * layer + 4, :] for i in range(2)], axis=0
            )
    for k in range(1, 4):
        for i in range(len(spans)):
            sum_copy(i, k).wait_send()
        last_zcopy(k, z).wait_send()
    for i in sent(ROUNDS - 1):
        wave_copy(ROUNDS - 1, i).wait_send()
    every(lambda k: last_copy(k, column_ahead(k), xy).wait_send())


def per_device(snapshots, reflect, courant, lags, owners):
    depth, rows, columns = courant.shape
    lines = depth * rows
    dma = pltpu.SemaphoreType.DMA
    any_space = pl.BlockSpec(memory_space=pl.ANY)
    scalars = pl.BlockSpec(memory_space=pltpu.SMEM)
    return pl.pallas_call(
        kernel,
        out_shape=jax.ShapeDtypeStruct(courant.shape, F32),
        in_specs=[any_space, any_space, any_space, scalars, scalars],
        out_specs=pl.BlockSpec(memory_space=pltpu.VMEM),
        scratch_shapes=[
            pltpu.VMEM((256, 256), BF16), pltpu.VMEM((OFFSETS, 256, 256), BF16), pltpu.VMEM((4, 64, 256), F32), dma((3,)),
            pltpu.VMEM((16, 16, 256), BF16), pltpu.VMEM((16, 16, 256), BF16), dma((16,)), dma((16,)),
            pltpu.VMEM((16, OFFSETS, 16, 256), BF16), pltpu.VMEM((16, OFFSETS, 16, 256), BF16),
            dma((CHUNKS, 16)), dma((CHUNKS, 16)), dma,
            pltpu.VMEM((8, 128), jnp.int32), pltpu.VMEM((16, 8, 128), jnp.int32), pltpu.SMEM((16, 8, 128), jnp.int32),
            dma((16,)), dma((16,)), dma,
            pltpu.VMEM((4, 16, 128), F32), pltpu.VMEM((16, 128), F32), pltpu.VMEM((4, 16, 128), F32), dma((4,)), dma((4,)),
            pltpu.VMEM((4, 128, 128), BF16), pltpu.VMEM((3, 128, 128), BF16), dma((3,)), dma((3,)),
            pltpu.VMEM((128, 128), BF16), pltpu.VMEM((4, 128, 128), BF16), dma((4,)), dma((4,)),
            pltpu.VMEM((128, 128), F32), pltpu.VMEM((4, 64, 128), F32), dma((3,)), dma((3,)),
            pltpu.VMEM((2 * LAG + 1, 128, 256), F32),
            pltpu.VMEM((4, 128, 128), F32), pltpu.VMEM((3, 128, 128), F32), dma((5, 3)), dma((5, 3)),
            pltpu.VMEM((ROUNDS, 2, 16, 128), F32), pltpu.VMEM((ROUNDS, 4, 2, 16, 128), F32),
            pltpu.VMEM((ROUNDS - 1, len(FAR), 16, 128), F32), dma((ROUNDS, len(NEAR))), dma((ROUNDS, len(NEAR))),
            pltpu.VMEM((4, 8, 128), F32), dma((3,)), dma((3,)),
            pltpu.VMEM((16, 16, 256), F32), dma((16,)), dma((16,)),
        ],
        compiler_params=pltpu.CompilerParams(
            collective_id=0, has_side_effects=True, vmem_limit_bytes=60 * 1024 * 1024
        ),
        name="born",
    )(
        snapshots.reshape(lines, columns),
        reflect.reshape(reflect.shape[0], lines, columns),
        courant,
        lags,
        owners,
    )


def solution(mesh):
    in_specs = (
        P("off", "dep", None, None),
        P("off", "dep", None, None),
        P("dep", None, None),
        P("off"),
        P(),
    )
    return jax.shard_map(
        per_device, mesh=mesh, in_specs=in_specs, out_specs=P("dep", None, None), check_vma=False
    )
```

```python
import jax
import jax.numpy as jnp
from jax import lax
from jax.experimental import pallas as pl
from jax.experimental.pallas import tpu as pltpu
from jax.sharding import PartitionSpec as P

ITERS = 8
LAG = 32
WEIGHTS = (-205.0 / 72.0, 8.0 / 5.0, -1.0 / 5.0, 8.0 / 315.0, -1.0 / 560.0)
MESH = pl.DeviceIdType.MESH
F32 = jnp.float32
BF16 = jnp.bfloat16
OFFSETS = 12
CHUNKS = 4
PART = OFFSETS // CHUNKS
FIRST = 2
STAR = ((-1, 0), (1, 0), (0, -1), (0, 1))
FAR = ((-2, 0), (2, 0), (0, -2), (0, 2), (-1, -1), (-1, 1), (1, -1), (1, 1))
NEAR = STAR + FAR
ROUNDS = 4


def rem(a, n):
    return lax.rem(a, jnp.int32(n))


def div(a, n):
    return lax.div(a, jnp.int32(n))


def snake(i):
    y, x = div(i, 4), rem(i, 4)
    return 4 * y + x + rem(y, 2) * (3 - 2 * x)


def inner(cur):
    row = lax.broadcasted_iota(jnp.int32, (8, 128), 0)
    line = rem(row, 4)
    c0, c1 = cur[:8], cur[8:]
    t0, t1 = pltpu.roll(c0, 4, 0), pltpu.roll(c1, 4, 0)
    both = jnp.where(row < 4, t0, t1)
    depth = (
        {1: both + jnp.where(row < 4, 0.0, t0), 2: c1, 3: jnp.where(row < 4, t1, 0.0)},
        {1: both + jnp.where(row < 4, t1, 0.0), 2: c0, 3: jnp.where(row < 4, 0.0, t0)},
    )
    out = []
    for half, c in enumerate((c0, c1)):
        total = (3.0 * WEIGHTS[0]) * c
        for k in range(1, 5):
            near = pltpu.roll(c, 128 - k, 1) + pltpu.roll(c, k, 1)
            if k < 4:
                near = near + depth[half][k]
                near = near + jnp.where(line < 4 - k, pltpu.roll(c, 8 - k, 0), 0.0)
                near = near + jnp.where(line >= k, pltpu.roll(c, k, 0), 0.0)
            total = total + WEIGHTS[k] * near
        out.append(total)
    return jnp.concatenate(out, axis=0)


def rim(side, tile):
    row = lax.broadcasted_iota(jnp.int32, (8, 128), 0)
    line = rem(row, 4)
    w = WEIGHTS
    a, b = tile[:8], tile[8:]
    if side[1] == 0:
        out = []
        for v in (a, b):
            total = w[4] * v
            for k in range(1, 4):
                if side[0] > 0:
                    total = total + w[k] * jnp.where(line < 4 - k, 0.0, pltpu.roll(v, 4 - k, 0))
                else:
                    total = total + w[k] * jnp.where(line < k, pltpu.roll(v, 4 + k, 0), 0.0)
            out.append(total)
        return jnp.concatenate(out, axis=0)
    ta, tb = pltpu.roll(a, 4, 0), pltpu.roll(b, 4, 0)
    both = jnp.where(row < 4, ta, tb)
    if side[1] > 0:
        last = jnp.where(row < 4, 0.0, ta)
        return jnp.concatenate(
            [w[3] * last + w[4] * a, w[1] * last + w[2] * a + w[3] * both + w[4] * b], axis=0
        )
    first = jnp.where(row < 4, tb, 0.0)
    return jnp.concatenate(
        [w[1] * first + w[2] * b + w[3] * both + w[4] * a, w[3] * first + w[4] * b], axis=0
    )


def windows(field):
    first, second = field[:, :128], field[:, 128:]
    lane = lax.broadcasted_iota(jnp.int32, first.shape, 1)
    f32, s32 = pltpu.roll(first, 32, 1), pltpu.roll(second, 32, 1)
    f96, s96 = pltpu.roll(first, 96, 1), pltpu.roll(second, 96, 1)
    return (
        jnp.where(lane < 32, 0.0, f32),
        jnp.where(lane < 96, f96, s96),
        jnp.where(lane < 32, f32, s32),
        jnp.where(lane < 96, s96, 0.0),
    )


def packed(top, bottom):
    lane = lax.broadcasted_iota(jnp.int32, top.shape, 1)
    return jnp.where(lane < 64, pltpu.roll(top, 96, 1), pltpu.roll(bottom, 32, 1))


def unpacked(a, b):
    lane = lax.broadcasted_iota(jnp.int32, a.shape, 1)
    return jnp.where(lane < 64, a, pltpu.roll(b, 64, 1)), jnp.where(lane < 64, pltpu.roll(a, 64, 1), b)


def kernel(
    snap_hbm, refl_hbm, cour_hbm, lags_ref, owners_ref, out_ref,
    snap_v, refl_v, cour_v, load_sem,
    snap_t, snap_r, snap_ss, snap_rs,
    refl_t, refl_r, refl_ss, refl_rs, own_sem,
    lag_v, lag_r, lag_s, lag_ss, lag_rs, lag_sem,
    cour_w, cour_s, cour_r, cour_ss, cour_rs,
    pick_s, pick_r, pick_ss, pick_rs,
    back_s, back_r, back_ss, back_rs,
    acc_w, acc_z, acc_zss, acc_zrs, moved,
    sum_s, sum_r, sum_ss, sum_rs,
    wave_s, wave_r, wave_f, wave_ss, wave_rs, term_ss, term_rs,
    last_z, last_zss, last_zrs,
    last, last_ss, last_rs,
):
    off = lax.axis_index("off")
    dep = lax.axis_index("dep")
    z, xy = rem(off, 4), div(off, 4)
    y, x = div(xy, 4), rem(xy, 4)
    block = snake(xy)

    loads = [
        pltpu.make_async_copy(snap_hbm, snap_v, load_sem.at[0]),
        pltpu.make_async_copy(refl_hbm, refl_v, load_sem.at[1]),
        pltpu.make_async_copy(cour_hbm, cour_v, load_sem.at[2]),
    ]
    for load in loads:
        load.start()

    def column_ahead(k):
        return rem(y + div(k, 4), 4) * 4 + rem(x + rem(k, 4), 4)

    def column_behind(k):
        return rem(y + 4 - div(k, 4), 4) * 4 + rem(x + 4 - rem(k, 4), 4)

    def in_plane(column):
        return {"off": column * 4 + z, "dep": dep}

    def in_column(z_to):
        return {"off": xy * 4 + z_to, "dep": dep}

    def beside(place):
        rows, layers = place
        return {"off": snake(rem(block + 16 + rows, 16)) * 4 + z, "dep": rem(dep + 8 + layers, 8)}

    def inside(place):
        b, d = block + place[0], dep + place[1]
        return jnp.where((b >= 0) & (b < 16) & (d >= 0) & (d < 8), 1.0, 0.0).astype(F32)

    def against(place):
        return (-place[0], -place[1])

    def remote(src, dst, send, recv, to):
        return pltpu.make_async_remote_copy(
            src_ref=src, dst_ref=dst, send_sem=send, recv_sem=recv, device_id=to, device_id_type=MESH
        )

    def each(lower, upper, body):
        def run(i, carry):
            body(i)
            return carry

        lax.fori_loop(lower, upper, run, 0)

    def every(body):
        for k in range(1, 16):
            body(jnp.int32(k))

    masks = {place: inside(place) for place in NEAR}
    barrier = pltpu.get_barrier_semaphore()

    def greet(to):
        pl.semaphore_signal(barrier, inc=1, device_id=to, device_id_type=MESH)

    every(lambda k: greet(in_plane(column_ahead(k))))
    for k in range(1, 4):
        greet(in_column(rem(z + k, 4)))
    met = [place for place in NEAR if place[1] != 0]
    for place in met:
        greet(beside(place))

    lane = lax.broadcasted_iota(jnp.int32, (8, 128), 1)
    lag_row = jnp.zeros((8, 128), jnp.int32)
    for h in range(OFFSETS):
        lag_row = jnp.where(lane == h, lags_ref[h], lag_row)
    lag_v[...] = lag_row
    lag_r[pl.ds(xy, 1)] = lag_row[None]

    to_row = lax.broadcasted_iota(jnp.int32, (256, 256), 0)
    from_row = lax.broadcasted_iota(jnp.int32, (256, 256), 1)
    wanted = rem(div(to_row, 4), 4) * 64 + div(to_row, 16) * 4 + rem(to_row, 4)
    order = jnp.where(from_row == wanted, 1.0, 0.0).astype(BF16)

    def ordered(image):
        return jnp.dot(order, image, preferred_element_type=F32).astype(BF16).reshape(16, 16, 256)

    loads[0].wait()
    snap_t[...] = ordered(snap_v[...])

    loads[1].wait()

    def order_one(h):
        refl_t[:, pl.ds(h, 1)] = ordered(refl_v[h])[:, None]

    each(0, PART, order_one)

    pl.semaphore_wait(barrier, 18 + len(met))
    def snap_copy(k, to, slot):
        return remote(snap_t.at[snake(to)], snap_r.at[slot], snap_ss.at[k], snap_rs.at[k], in_plane(to))

    def lag_copy(k, to, slot):
        return remote(lag_v, lag_r.at[slot], lag_ss.at[k], lag_rs.at[k], in_plane(to))

    def refl_copy(part, k, to, slot):
        return remote(
            refl_t.at[snake(to), pl.ds(part * PART, PART)],
            refl_r.at[slot, pl.ds(part * PART, PART)],
            refl_ss.at[part, k],
            refl_rs.at[part, k],
            in_plane(to),
        )

    every(lambda k: snap_copy(k, column_ahead(k), xy).start())
    snap_r[pl.ds(xy, 1)] = snap_t[pl.ds(block, 1)]
    def send_part(part):
        if part:
            each(part * PART, (part + 1) * PART, order_one)
        every(lambda k: refl_copy(part, k, column_ahead(k), xy).start())

    for part in (0, 1):
        send_part(part)
    every(lambda k: lag_copy(k, column_ahead(k), xy).start())
    loads[2].wait()
    odd = rem(block, 2)
    layers = []
    for layer in range(4):
        rows = cour_v[layer, pl.ds(pl.multiple_of(8 * div(block, 2), 8), 8), :]
        layers.append(jnp.where(odd == 0, rows[:4], rows[4:]))
    for q, window in enumerate(windows(jnp.concatenate(layers, axis=0))):
        cour_w[q] = window
    courant = cour_w[z]
    cour_s[...] = courant

    def cour_copy(i):
        return remote(cour_s, cour_r.at[i], cour_ss.at[i], cour_rs.at[i], beside(against(STAR[i])))

    for i in range(4):
        cour_copy(i).start()
    every(lambda k: snap_copy(k, xy, column_behind(k)).wait_recv())
    for t in range(ITERS):
        owner = owners_ref[t]
        kept = jnp.where(rem(owner, 4) == z, 1.0, 0.0).astype(F32)
        field = snap_r[div(owner, 4)].astype(F32) * kept
        for q, window in enumerate(windows(field)):
            pick_s[q, 16 * t : 16 * t + 16, :] = window.astype(BF16)

    def pick_copy(k):
        z_to = rem(z + k, 4)
        return remote(pick_s.at[z_to], pick_r.at[k - 1], pick_ss.at[k - 1], pick_rs.at[k - 1], in_column(z_to))

    for k in range(1, 4):
        pick_copy(k).start()
    back = pick_s[z].astype(F32)
    for k in range(1, 4):
        pick_copy(k).wait_recv()
        back = back + pick_r[k - 1].astype(F32)
    back_s[...] = back.astype(BF16)
    def back_copy(i):
        return remote(back_s, back_r.at[i], back_ss.at[i], back_rs.at[i], beside(against(STAR[i])))

    for i in reversed(range(4)):
        back_copy(i).start()
    send_part(2)
    for i in range(4):
        back_copy(i).wait_recv()

    def accelerate(i):
        for j in range(4):
            rows = pl.ds(pl.multiple_of(64 * i + 16 * j, 16), 16)
            total = inner(back_s[rows, :].astype(F32))
            for n, side in enumerate(STAR):
                total = total + rim(side, back_r[n, rows, :].astype(F32)) * masks[side]
            acc_w[rows, :] = courant * total

    each(0, ITERS // 4, accelerate)
    acc_z[pl.ds(z, 1)] = packed(acc_w[:64, :], acc_w[64:, :])[None]
    def acc_zcopy(k, slot):
        return remote(acc_z.at[slot], acc_z.at[slot], acc_zss.at[k - 1], acc_zrs.at[k - 1], in_column(rem(z + k, 4)))

    for k in range(1, 4):
        acc_zcopy(k, z).start()
    send_part(3)
    own = pltpu.make_async_copy(refl_t.at[block], refl_r.at[xy], own_sem)
    own.start()
    for k in range(1, 4):
        acc_zcopy(k, rem(z + 4 - k, 4)).wait_recv()
    first = jnp.concatenate(unpacked(acc_z[0], acc_z[1]), axis=0)
    second = jnp.concatenate(unpacked(acc_z[2], acc_z[3]), axis=0)

    def move_all(rows, unrolled):
        a, b = first[rows], second[rows]
        wide = lax.broadcasted_iota(jnp.int32, a.shape, 1)
        moved[LAG, rows, :128] = a
        moved[LAG, rows, 128:] = b

        def move(i):
            for j in range(1, unrolled + 1):
                lag = unrolled * i + j
                ra, rb = pltpu.roll(a, lag, 1), pltpu.roll(b, lag, 1)
                moved[LAG + lag, rows, :128] = jnp.where(wide < lag, 0.0, ra)
                moved[LAG + lag, rows, 128:] = jnp.where(wide < lag, ra, rb)
                rest = 128 - lag
                ra, rb = pltpu.roll(a, rest, 1), pltpu.roll(b, rest, 1)
                moved[LAG - lag, rows, :128] = jnp.where(wide < rest, ra, rb)
                moved[LAG - lag, rows, 128:] = jnp.where(wide < rest, rb, 0.0)

        each(0, LAG // unrolled, move)

    def add_parts(steps, ready):
        sums = tuple(jnp.zeros((16, 256), F32) for _ in steps)
        for part in range(CHUNKS):
            ready(part)

            def add_device(s, sums):
                sums = list(sums)
                for h in range(part * PART, (part + 1) * PART):
                    image = refl_r[s, h].astype(F32)
                    place = lag_s[s, 0, h] + LAG
                    for i, t in enumerate(steps):
                        sums[i] = sums[i] + image * moved[place, 16 * t : 16 * t + 16, :]
                return tuple(sums)

            sums = lax.fori_loop(0, 16, add_device, sums)
        for i, t in enumerate(steps):
            for q, window in enumerate(windows(sums[i])):
                sum_s[q, 16 * t : 16 * t + 16, :] = window

    def arrive(part):
        every(lambda k: refl_copy(part, k, xy, column_behind(k)).wait_recv())

    own.wait()
    every(lambda k: lag_copy(k, xy, column_behind(k)).wait_recv())
    scalars = pltpu.make_async_copy(lag_r, lag_s, lag_sem)
    scalars.start()
    scalars.wait()
    move_all(slice(0, 16 * FIRST), 8)
    add_parts(range(FIRST), arrive)
    spans = ((0, FIRST), (FIRST, 1), (FIRST + 1, 2), (FIRST + 3, 2), (FIRST + 5, 1))

    def sum_copy(i, k):
        z_to = rem(z + k, 4)
        rows = pl.ds(16 * spans[i][0], 16 * spans[i][1])
        return remote(
            sum_s.at[z_to, rows, :], sum_r.at[k - 1, rows, :], sum_ss.at[i, k - 1], sum_rs.at[i, k - 1], in_column(z_to)
        )

    for k in range(1, 4):
        sum_copy(0, k).start()
    move_all(slice(16 * FIRST, 16 * ITERS), 4)
    add_parts(range(FIRST, ITERS), lambda part: None)
    for k in range(1, 4):
        sum_copy(1, k).start()

    every(lambda k: snap_copy(k, column_ahead(k), xy).wait_send())
    every(lambda k: lag_copy(k, column_ahead(k), xy).wait_send())
    for part in range(CHUNKS):
        every(lambda k: refl_copy(part, k, column_ahead(k), xy).wait_send())
    for k in range(1, 4):
        pick_copy(k).wait_send()
        acc_zcopy(k, z).wait_send()
    for i in range(4):
        back_copy(i).wait_send()
        cour_copy(i).wait_send()
    for k in range(1, 4):
        sum_copy(0, k).wait_recv()

    def source(t):
        rows = slice(16 * t, 16 * t + 16)
        return sum_s[z, rows, :] + sum_r[0, rows, :] + sum_r[1, rows, :] + sum_r[2, rows, :]

    for i in range(4):
        cour_copy(i).wait_recv()

    def wave_copy(r, i):
        to = beside(against(NEAR[i]))
        if i < 4:
            return remote(wave_s.at[r, 0], wave_r.at[r, i, 0], wave_ss.at[r, i], wave_rs.at[r, i], to)
        return remote(wave_s.at[r, 0], wave_f.at[r, i - 4], wave_ss.at[r, i], wave_rs.at[r, i], to)

    def term_copy(r, i):
        to = beside(against(STAR[i]))
        return remote(wave_s.at[r, 1], wave_r.at[r, i, 1], term_ss.at[r, i], term_rs.at[r, i], to)

    def sent(r):
        return range(len(NEAR) if r < ROUNDS - 1 else 4)

    def at(a, b):
        return (a[0] + b[0], a[1] + b[1])

    here = (0, 0)
    old = {place: jnp.zeros((16, 128), F32) for place in (here,) + STAR}
    wave = source(0)
    courants = {here: courant}
    for i, place in enumerate(STAR):
        courants[place] = cour_r[i] * masks[place]
    for r in range(ROUNDS):
        more = r < ROUNDS - 1
        wave_s[r, 0] = wave
        for i in (11, 10, 9, 8, 7, 6, 3, 2, 5, 4, 1, 0):
            if i in sent(r):
                wave_copy(r, i).start()
        now = source(2 * r + 1)
        if more:
            wave_s[r, 1] = now
            for i in (3, 2, 1, 0):
                term_copy(r, i).start()
        if more:
            for k in range(1, 4):
                sum_copy(2 + r, k).start()
        if r:
            for i in sent(r - 1):
                wave_copy(r - 1, i).wait_send()
            for i in range(4):
                term_copy(r - 1, i).wait_send()
        slope = {here: inner(wave)}
        base = {here: 2.0 * wave - old[here] + now}
        if more:
            for side in STAR:
                slope[side] = rim(against(side), wave)
        for i in (0, 1, 4, 5, 2, 3, 6, 7, 8, 9, 10, 11):
            if i not in sent(r):
                continue
            wave_copy(r, i).wait_recv()
            place = NEAR[i]
            tile = (wave_r[r, i, 0] if i < 4 else wave_f[r, i - 4]) * masks[place]
            for side in STAR:
                to = at(place, against(side))
                if to in slope and (to != place) and (more or to == here):
                    slope[to] = slope[to] + rim(side, tile)
            if i < 4 and more:
                slope[place] = slope[place] + inner(tile)
                base[place] = 2.0 * tile - old[place]
        for i in range(4 if more else 0):
            term_copy(r, i).wait_recv()
            base[STAR[i]] = base[STAR[i]] + wave_r[r, i, 1] * masks[STAR[i]]
        ahead = {place: base[place] + courants[place] * slope[place] for place in base}
        if not more:
            wave = ahead[here]
            break
        for i in (1, 2) if r == 0 else (2 + r,):
            for k in range(1, 4):
                sum_copy(i, k).wait_recv()
        total = inner(ahead[here])
        for side in STAR:
            total = total + rim(side, ahead[side])
        wave = 2.0 * ahead[here] - wave + courant * total + source(2 * r + 2)
        old = ahead
    last_z[0] = packed(wave[:8], wave[8:])

    def last_zcopy(k):
        return remote(last_z.at[0], last_z.at[k], last_zss.at[k - 1], last_zrs.at[k - 1], in_column(rem(z + k, 4)))

    def last_copy(i, k, to, column):
        slots = pl.ds(0, 1) if i == 0 else pl.ds(1, 3)
        return remote(last_z.at[slots], last.at[snake(column), slots], last_ss.at[i, k], last_rs.at[i, k], in_plane(to))

    for k in range(1, 4):
        last_zcopy(k).start()
    every(lambda k: last_copy(0, k, column_ahead(k), xy).start())
    for k in range(1, 4):
        for i in range(len(spans)):
            sum_copy(i, k).wait_send()
    for i in sent(ROUNDS - 1):
        wave_copy(ROUNDS - 1, i).wait_send()
    for k in range(1, 4):
        last_zcopy(k).wait_recv()
    every(lambda k: last_copy(1, k, column_ahead(k), xy).start())
    last[pl.ds(block, 1)] = last_z[...][None]
    every(lambda k: last_copy(0, k, xy, column_behind(k)).wait_recv())
    every(lambda k: last_copy(1, k, xy, column_behind(k)).wait_recv())

    def quarter(place, q):
        return last[place, pl.ds(rem(z - q + 4, 4), 1)][0]

    for pair in range(8):
        slabs = []
        for place in (2 * pair, 2 * pair + 1):
            west = unpacked(quarter(place, 0), quarter(place, 1))
            east = unpacked(quarter(place, 2), quarter(place, 3))
            slabs.append([jnp.concatenate([west[half], east[half]], axis=1) for half in range(2)])
        for layer in range(4):
            rows = slice(4 * (layer % 2), 4 * (layer % 2) + 4)
            out_ref[layer, 8 * pair : 8 * pair + 8, :] = jnp.concatenate(
                [slab[layer // 2][rows] for slab in slabs], axis=0
            )
    for k in range(1, 4):
        last_zcopy(k).wait_send()
    for i in range(2):
        every(lambda k: last_copy(i, k, column_ahead(k), xy).wait_send())


def per_device(snapshots, reflect, courant, lags, owners):
    depth, rows, columns = courant.shape
    lines = depth * rows
    dma = pltpu.SemaphoreType.DMA
    any_space = pl.BlockSpec(memory_space=pl.ANY)
    scalars = pl.BlockSpec(memory_space=pltpu.SMEM)
    return pl.pallas_call(
        kernel,
        out_shape=jax.ShapeDtypeStruct(courant.shape, F32),
        in_specs=[any_space, any_space, any_space, scalars, scalars],
        out_specs=pl.BlockSpec(memory_space=pltpu.VMEM),
        scratch_shapes=[
            pltpu.VMEM((256, 256), BF16), pltpu.VMEM((OFFSETS, 256, 256), BF16), pltpu.VMEM((4, 64, 256), F32), dma((3,)),
            pltpu.VMEM((16, 16, 256), BF16), pltpu.VMEM((16, 16, 256), BF16), dma((16,)), dma((16,)),
            pltpu.VMEM((16, OFFSETS, 16, 256), BF16), pltpu.VMEM((16, OFFSETS, 16, 256), BF16),
            dma((CHUNKS, 16)), dma((CHUNKS, 16)), dma,
            pltpu.VMEM((8, 128), jnp.int32), pltpu.VMEM((16, 8, 128), jnp.int32), pltpu.SMEM((16, 8, 128), jnp.int32),
            dma((16,)), dma((16,)), dma,
            pltpu.VMEM((4, 16, 128), F32), pltpu.VMEM((16, 128), F32), pltpu.VMEM((4, 16, 128), F32), dma((4,)), dma((4,)),
            pltpu.VMEM((4, 128, 128), BF16), pltpu.VMEM((3, 128, 128), BF16), dma((3,)), dma((3,)),
            pltpu.VMEM((128, 128), BF16), pltpu.VMEM((4, 128, 128), BF16), dma((4,)), dma((4,)),
            pltpu.VMEM((128, 128), F32), pltpu.VMEM((4, 64, 128), F32), dma((3,)), dma((3,)),
            pltpu.VMEM((2 * LAG + 1, 128, 256), F32),
            pltpu.VMEM((4, 128, 128), F32), pltpu.VMEM((3, 128, 128), F32), dma((5, 3)), dma((5, 3)),
            pltpu.VMEM((ROUNDS, 2, 16, 128), F32), pltpu.VMEM((ROUNDS, 4, 2, 16, 128), F32),
            pltpu.VMEM((ROUNDS - 1, len(FAR), 16, 128), F32), dma((ROUNDS, len(NEAR))), dma((ROUNDS, len(NEAR))),
            dma((ROUNDS - 1, 4)), dma((ROUNDS - 1, 4)),
            pltpu.VMEM((4, 8, 128), F32), dma((3,)), dma((3,)),
            pltpu.VMEM((16, 4, 8, 128), F32), dma((2, 16)), dma((2, 16)),
        ],
        compiler_params=pltpu.CompilerParams(
            collective_id=0, has_side_effects=True, vmem_limit_bytes=60 * 1024 * 1024
        ),
        name="born",
    )(
        snapshots.reshape(lines, columns),
        reflect.reshape(reflect.shape[0], lines, columns),
        courant,
        lags,
        owners,
    )


def solution(mesh):
    in_specs = (
        P("off", "dep", None, None),
        P("off", "dep", None, None),
        P("dep", None, None),
        P("off"),
        P(),
    )
    return jax.shard_map(
        per_device, mesh=mesh, in_specs=in_specs, out_specs=P("dep", None, None), check_vma=False
    )
```

```python
import jax
import jax.numpy as jnp
from jax import lax
from jax.experimental import pallas as pl
from jax.experimental.pallas import tpu as pltpu
from jax.sharding import PartitionSpec as P

ITERS = 8
LAG = 32
WEIGHTS = (-205.0 / 72.0, 8.0 / 5.0, -1.0 / 5.0, 8.0 / 315.0, -1.0 / 560.0)
MESH = pl.DeviceIdType.MESH
F32 = jnp.float32
BF16 = jnp.bfloat16
OFFSETS = 12
CHUNKS = 4
PART = OFFSETS // CHUNKS
FIRST = 2
STAR = ((-1, 0), (1, 0), (0, -1), (0, 1))
FAR = ((-2, 0), (2, 0), (0, -2), (0, 2), (-1, -1), (-1, 1), (1, -1), (1, 1))
NEAR = STAR + FAR
ROUNDS = 4


def rem(a, n):
    return lax.rem(a, jnp.int32(n))


def div(a, n):
    return lax.div(a, jnp.int32(n))


def snake(i):
    y, x = div(i, 4), rem(i, 4)
    return 4 * y + x + rem(y, 2) * (3 - 2 * x)


def inner(cur):
    row = lax.broadcasted_iota(jnp.int32, (8, 128), 0)
    line = rem(row, 4)
    c0, c1 = cur[:8], cur[8:]
    t0, t1 = pltpu.roll(c0, 4, 0), pltpu.roll(c1, 4, 0)
    both = jnp.where(row < 4, t0, t1)
    depth = (
        {1: both + jnp.where(row < 4, 0.0, t0), 2: c1, 3: jnp.where(row < 4, t1, 0.0)},
        {1: both + jnp.where(row < 4, t1, 0.0), 2: c0, 3: jnp.where(row < 4, 0.0, t0)},
    )
    out = []
    for half, c in enumerate((c0, c1)):
        total = (3.0 * WEIGHTS[0]) * c
        for k in range(1, 5):
            near = pltpu.roll(c, 128 - k, 1) + pltpu.roll(c, k, 1)
            if k < 4:
                near = near + depth[half][k]
                near = near + jnp.where(line < 4 - k, pltpu.roll(c, 8 - k, 0), 0.0)
                near = near + jnp.where(line >= k, pltpu.roll(c, k, 0), 0.0)
            total = total + WEIGHTS[k] * near
        out.append(total)
    return jnp.concatenate(out, axis=0)


def rim(side, tile):
    row = lax.broadcasted_iota(jnp.int32, (8, 128), 0)
    line = rem(row, 4)
    w = WEIGHTS
    a, b = tile[:8], tile[8:]
    if side[1] == 0:
        out = []
        for v in (a, b):
            total = w[4] * v
            for k in range(1, 4):
                if side[0] > 0:
                    total = total + w[k] * jnp.where(line < 4 - k, 0.0, pltpu.roll(v, 4 - k, 0))
                else:
                    total = total + w[k] * jnp.where(line < k, pltpu.roll(v, 4 + k, 0), 0.0)
            out.append(total)
        return jnp.concatenate(out, axis=0)
    ta, tb = pltpu.roll(a, 4, 0), pltpu.roll(b, 4, 0)
    both = jnp.where(row < 4, ta, tb)
    if side[1] > 0:
        last = jnp.where(row < 4, 0.0, ta)
        return jnp.concatenate(
            [w[3] * last + w[4] * a, w[1] * last + w[2] * a + w[3] * both + w[4] * b], axis=0
        )
    first = jnp.where(row < 4, tb, 0.0)
    return jnp.concatenate(
        [w[1] * first + w[2] * b + w[3] * both + w[4] * a, w[3] * first + w[4] * b], axis=0
    )


def windows(field):
    first, second = field[:, :128], field[:, 128:]
    lane = lax.broadcasted_iota(jnp.int32, first.shape, 1)
    f32, s32 = pltpu.roll(first, 32, 1), pltpu.roll(second, 32, 1)
    f96, s96 = pltpu.roll(first, 96, 1), pltpu.roll(second, 96, 1)
    return (
        jnp.where(lane < 32, 0.0, f32),
        jnp.where(lane < 96, f96, s96),
        jnp.where(lane < 32, f32, s32),
        jnp.where(lane < 96, s96, 0.0),
    )


def packed(top, bottom):
    lane = lax.broadcasted_iota(jnp.int32, top.shape, 1)
    return jnp.where(lane < 64, pltpu.roll(top, 96, 1), pltpu.roll(bottom, 32, 1))


def unpacked(a, b):
    lane = lax.broadcasted_iota(jnp.int32, a.shape, 1)
    return jnp.where(lane < 64, a, pltpu.roll(b, 64, 1)), jnp.where(lane < 64, pltpu.roll(a, 64, 1), b)


def kernel(
    snap_hbm, refl_hbm, cour_hbm, lags_ref, owners_ref, out_ref,
    snap_v, refl_v, cour_v, load_sem,
    snap_t, snap_r, snap_ss, snap_rs,
    refl_t, refl_r, refl_ss, refl_rs, own_sem,
    lag_v, lag_r, lag_s, lag_ss, lag_rs, lag_sem,
    cour_w, cour_s, cour_r, cour_ss, cour_rs,
    pick_s, pick_r, pick_ss, pick_rs,
    back_s, back_r, back_ss, back_rs,
    acc_w, acc_z, acc_zss, acc_zrs, moved,
    sum_s, sum_r, sum_ss, sum_rs,
    wave_s, wave_r, wave_f, wave_ss, wave_rs, term_ss, term_rs,
    last_z, last_zss, last_zrs,
    last, last_ss, last_rs,
):
    off = lax.axis_index("off")
    dep = lax.axis_index("dep")
    z, xy = rem(off, 4), div(off, 4)
    y, x = div(xy, 4), rem(xy, 4)
    block = snake(xy)

    loads = [
        pltpu.make_async_copy(snap_hbm, snap_v, load_sem.at[0]),
        pltpu.make_async_copy(refl_hbm, refl_v, load_sem.at[1]),
        pltpu.make_async_copy(cour_hbm, cour_v, load_sem.at[2]),
    ]
    for load in loads:
        load.start()

    def column_ahead(k):
        return rem(y + div(k, 4), 4) * 4 + rem(x + rem(k, 4), 4)

    def column_behind(k):
        return rem(y + 4 - div(k, 4), 4) * 4 + rem(x + 4 - rem(k, 4), 4)

    def in_plane(column):
        return {"off": column * 4 + z, "dep": dep}

    def in_column(z_to):
        return {"off": xy * 4 + z_to, "dep": dep}

    def beside(place):
        rows, layers = place
        return {"off": snake(rem(block + 16 + rows, 16)) * 4 + z, "dep": rem(dep + 8 + layers, 8)}

    def inside(place):
        b, d = block + place[0], dep + place[1]
        return jnp.where((b >= 0) & (b < 16) & (d >= 0) & (d < 8), 1.0, 0.0).astype(F32)

    def against(place):
        return (-place[0], -place[1])

    def remote(src, dst, send, recv, to):
        return pltpu.make_async_remote_copy(
            src_ref=src, dst_ref=dst, send_sem=send, recv_sem=recv, device_id=to, device_id_type=MESH
        )

    def each(lower, upper, body):
        def run(i, carry):
            body(i)
            return carry

        lax.fori_loop(lower, upper, run, 0)

    def every(body):
        for k in range(1, 16):
            body(jnp.int32(k))

    masks = {place: inside(place) for place in NEAR}
    barrier = pltpu.get_barrier_semaphore()

    def greet(to):
        pl.semaphore_signal(barrier, inc=1, device_id=to, device_id_type=MESH)

    every(lambda k: greet(in_plane(column_ahead(k))))
    for k in range(1, 4):
        greet(in_column(rem(z + k, 4)))
    met = [place for place in NEAR if place[1] != 0]
    for place in met:
        greet(beside(place))

    lane = lax.broadcasted_iota(jnp.int32, (8, 128), 1)
    lag_row = jnp.zeros((8, 128), jnp.int32)
    for h in range(OFFSETS):
        lag_row = jnp.where(lane == h, lags_ref[h], lag_row)
    lag_v[...] = lag_row
    lag_r[pl.ds(xy, 1)] = lag_row[None]

    to_row = lax.broadcasted_iota(jnp.int32, (256, 256), 0)
    from_row = lax.broadcasted_iota(jnp.int32, (256, 256), 1)
    wanted = rem(div(to_row, 4), 4) * 64 + div(to_row, 16) * 4 + rem(to_row, 4)
    order = jnp.where(from_row == wanted, 1.0, 0.0).astype(BF16)

    def ordered(image):
        return jnp.dot(order, image, preferred_element_type=F32).astype(BF16).reshape(16, 16, 256)

    loads[0].wait()
    snap_t[...] = ordered(snap_v[...])

    loads[1].wait()

    def order_one(h):
        refl_t[:, pl.ds(h, 1)] = ordered(refl_v[h])[:, None]

    each(0, PART, order_one)

    pl.semaphore_wait(barrier, 18 + len(met))
    def snap_copy(k, to, slot):
        return remote(snap_t.at[snake(to)], snap_r.at[slot], snap_ss.at[k], snap_rs.at[k], in_plane(to))

    def lag_copy(k, to, slot):
        return remote(lag_v, lag_r.at[slot], lag_ss.at[k], lag_rs.at[k], in_plane(to))

    def refl_copy(part, k, to, slot):
        return remote(
            refl_t.at[snake(to), pl.ds(part * PART, PART)],
            refl_r.at[slot, pl.ds(part * PART, PART)],
            refl_ss.at[part, k],
            refl_rs.at[part, k],
            in_plane(to),
        )

    every(lambda k: snap_copy(k, column_ahead(k), xy).start())
    snap_r[pl.ds(xy, 1)] = snap_t[pl.ds(block, 1)]
    def send_part(part):
        if part:
            each(part * PART, (part + 1) * PART, order_one)
        every(lambda k: refl_copy(part, k, column_ahead(k), xy).start())

    for part in (0, 1):
        send_part(part)
    every(lambda k: lag_copy(k, column_ahead(k), xy).start())
    loads[2].wait()
    odd = rem(block, 2)
    layers = []
    for layer in range(4):
        rows = cour_v[layer, pl.ds(pl.multiple_of(8 * div(block, 2), 8), 8), :]
        layers.append(jnp.where(odd == 0, rows[:4], rows[4:]))
    for q, window in enumerate(windows(jnp.concatenate(layers, axis=0))):
        cour_w[q] = window
    courant = cour_w[z]
    cour_s[...] = courant

    def cour_copy(i):
        return remote(cour_s, cour_r.at[i], cour_ss.at[i], cour_rs.at[i], beside(against(STAR[i])))

    for i in range(4):
        cour_copy(i).start()
    every(lambda k: snap_copy(k, xy, column_behind(k)).wait_recv())
    for t in range(ITERS):
        owner = owners_ref[t]
        kept = jnp.where(rem(owner, 4) == z, 1.0, 0.0).astype(F32)
        field = snap_r[div(owner, 4)].astype(F32) * kept
        for q, window in enumerate(windows(field)):
            pick_s[q, 16 * t : 16 * t + 16, :] = window.astype(BF16)

    def pick_copy(k):
        z_to = rem(z + k, 4)
        return remote(pick_s.at[z_to], pick_r.at[k - 1], pick_ss.at[k - 1], pick_rs.at[k - 1], in_column(z_to))

    for k in range(1, 4):
        pick_copy(k).start()
    back = pick_s[z].astype(F32)
    for k in range(1, 4):
        pick_copy(k).wait_recv()
        back = back + pick_r[k - 1].astype(F32)
    back_s[...] = back.astype(BF16)
    def back_copy(i):
        return remote(back_s, back_r.at[i], back_ss.at[i], back_rs.at[i], beside(against(STAR[i])))

    for i in reversed(range(4)):
        back_copy(i).start()
    send_part(2)
    for i in range(4):
        back_copy(i).wait_recv()

    def accelerate(i):
        for j in range(4):
            rows = pl.ds(pl.multiple_of(64 * i + 16 * j, 16), 16)
            total = inner(back_s[rows, :].astype(F32))
            for n, side in enumerate(STAR):
                total = total + rim(side, back_r[n, rows, :].astype(F32)) * masks[side]
            acc_w[rows, :] = courant * total

    for i in range(ITERS // 4):
        accelerate(i)
    acc_z[pl.ds(z, 1)] = packed(acc_w[:64, :], acc_w[64:, :])[None]
    def acc_zcopy(k, slot):
        return remote(acc_z.at[slot], acc_z.at[slot], acc_zss.at[k - 1], acc_zrs.at[k - 1], in_column(rem(z + k, 4)))

    for k in range(1, 4):
        acc_zcopy(k, z).start()
    send_part(3)
    own = pltpu.make_async_copy(refl_t.at[block], refl_r.at[xy], own_sem)
    own.start()
    for k in range(1, 4):
        acc_zcopy(k, rem(z + 4 - k, 4)).wait_recv()
    first = jnp.concatenate(unpacked(acc_z[0], acc_z[1]), axis=0)
    second = jnp.concatenate(unpacked(acc_z[2], acc_z[3]), axis=0)

    def move_all(rows, unrolled):
        a, b = first[rows], second[rows]
        wide = lax.broadcasted_iota(jnp.int32, a.shape, 1)
        moved[LAG, rows, :128] = a
        moved[LAG, rows, 128:] = b

        def move(i):
            for j in range(1, unrolled + 1):
                lag = unrolled * i + j
                ra, rb = pltpu.roll(a, lag, 1), pltpu.roll(b, lag, 1)
                moved[LAG + lag, rows, :128] = jnp.where(wide < lag, 0.0, ra)
                moved[LAG + lag, rows, 128:] = jnp.where(wide < lag, ra, rb)
                rest = 128 - lag
                ra, rb = pltpu.roll(a, rest, 1), pltpu.roll(b, rest, 1)
                moved[LAG - lag, rows, :128] = jnp.where(wide < rest, ra, rb)
                moved[LAG - lag, rows, 128:] = jnp.where(wide < rest, rb, 0.0)

        each(0, LAG // unrolled, move)

    def add_parts(steps, ready):
        sums = tuple(jnp.zeros((16, 256), F32) for _ in steps)
        for part in range(CHUNKS):
            ready(part)

            def add_device(s, sums):
                sums = list(sums)
                for h in range(part * PART, (part + 1) * PART):
                    image = refl_r[s, h].astype(F32)
                    place = lag_s[s, 0, h] + LAG
                    for i, t in enumerate(steps):
                        sums[i] = sums[i] + image * moved[place, 16 * t : 16 * t + 16, :]
                return tuple(sums)

            sums = lax.fori_loop(0, 16, add_device, sums)
        for i, t in enumerate(steps):
            for q, window in enumerate(windows(sums[i])):
                sum_s[q, 16 * t : 16 * t + 16, :] = window

    def arrive(part):
        every(lambda k: refl_copy(part, k, xy, column_behind(k)).wait_recv())

    own.wait()
    every(lambda k: lag_copy(k, xy, column_behind(k)).wait_recv())
    scalars = pltpu.make_async_copy(lag_r, lag_s, lag_sem)
    scalars.start()
    scalars.wait()
    move_all(slice(0, 16 * FIRST), 8)
    add_parts(range(FIRST), arrive)
    spans = ((0, FIRST), (FIRST, 1), (FIRST + 1, 2), (FIRST + 3, 2), (FIRST + 5, 1))

    def sum_copy(i, k):
        z_to = rem(z + k, 4)
        rows = pl.ds(16 * spans[i][0], 16 * spans[i][1])
        return remote(
            sum_s.at[z_to, rows, :], sum_r.at[k - 1, rows, :], sum_ss.at[i, k - 1], sum_rs.at[i, k - 1], in_column(z_to)
        )

    for k in range(1, 4):
        sum_copy(0, k).start()
    move_all(slice(16 * FIRST, 16 * ITERS), 4)
    add_parts(range(FIRST, ITERS), lambda part: None)
    for k in range(1, 4):
        sum_copy(1, k).start()

    every(lambda k: snap_copy(k, column_ahead(k), xy).wait_send())
    every(lambda k: lag_copy(k, column_ahead(k), xy).wait_send())
    for part in range(CHUNKS):
        every(lambda k: refl_copy(part, k, column_ahead(k), xy).wait_send())
    for k in range(1, 4):
        pick_copy(k).wait_send()
        acc_zcopy(k, z).wait_send()
    for i in range(4):
        back_copy(i).wait_send()
        cour_copy(i).wait_send()
    for k in range(1, 4):
        sum_copy(0, k).wait_recv()

    def source(t):
        rows = slice(16 * t, 16 * t + 16)
        return sum_s[z, rows, :] + sum_r[0, rows, :] + sum_r[1, rows, :] + sum_r[2, rows, :]

    for i in range(4):
        cour_copy(i).wait_recv()

    def wave_copy(r, i):
        to = beside(against(NEAR[i]))
        if i < 4:
            return remote(wave_s.at[r, 0], wave_r.at[r, i, 0], wave_ss.at[r, i], wave_rs.at[r, i], to)
        return remote(wave_s.at[r, 0], wave_f.at[r, i - 4], wave_ss.at[r, i], wave_rs.at[r, i], to)

    def term_copy(r, i):
        to = beside(against(STAR[i]))
        return remote(wave_s.at[r, 1], wave_r.at[r, i, 1], term_ss.at[r, i], term_rs.at[r, i], to)

    def sent(r):
        return range(len(NEAR) if r < ROUNDS - 1 else 4)

    def at(a, b):
        return (a[0] + b[0], a[1] + b[1])

    here = (0, 0)
    old = {place: jnp.zeros((16, 128), F32) for place in (here,) + STAR}
    wave = source(0)
    courants = {here: courant}
    for i, place in enumerate(STAR):
        courants[place] = cour_r[i] * masks[place]
    for r in range(ROUNDS):
        more = r < ROUNDS - 1
        wave_s[r, 0] = wave
        for i in (11, 10, 9, 8, 7, 6, 3, 2, 5, 4, 1, 0):
            if i in sent(r):
                wave_copy(r, i).start()
        now = source(2 * r + 1)
        if more:
            wave_s[r, 1] = now
            for i in (3, 2, 1, 0):
                term_copy(r, i).start()
        if more:
            for k in range(1, 4):
                sum_copy(2 + r, k).start()
        if r:
            for i in sent(r - 1):
                wave_copy(r - 1, i).wait_send()
            for i in range(4):
                term_copy(r - 1, i).wait_send()
        slope = {here: inner(wave)}
        base = {here: 2.0 * wave - old[here] + now}
        if more:
            for side in STAR:
                slope[side] = rim(against(side), wave)
        for i in (0, 1, 4, 5, 2, 3, 6, 7, 8, 9, 10, 11):
            if i not in sent(r):
                continue
            wave_copy(r, i).wait_recv()
            place = NEAR[i]
            tile = (wave_r[r, i, 0] if i < 4 else wave_f[r, i - 4]) * masks[place]
            for side in STAR:
                to = at(place, against(side))
                if to in slope and (to != place) and (more or to == here):
                    slope[to] = slope[to] + rim(side, tile)
            if i < 4 and more:
                slope[place] = slope[place] + inner(tile)
                base[place] = 2.0 * tile - old[place]
        for i in range(4 if more else 0):
            term_copy(r, i).wait_recv()
            base[STAR[i]] = base[STAR[i]] + wave_r[r, i, 1] * masks[STAR[i]]
        ahead = {place: base[place] + courants[place] * slope[place] for place in base}
        if not more:
            wave = ahead[here]
            break
        for i in (1, 2) if r == 0 else (2 + r,):
            for k in range(1, 4):
                sum_copy(i, k).wait_recv()
        total = inner(ahead[here])
        for side in STAR:
            total = total + rim(side, ahead[side])
        wave = 2.0 * ahead[here] - wave + courant * total + source(2 * r + 2)
        old = ahead
    last_z[0] = packed(wave[:8], wave[8:])

    def last_zcopy(k):
        return remote(last_z.at[0], last_z.at[k], last_zss.at[k - 1], last_zrs.at[k - 1], in_column(rem(z + k, 4)))

    def last_copy(i, k, to, column):
        slots = pl.ds(0, 1) if i == 0 else pl.ds(1, 3)
        return remote(last_z.at[slots], last.at[snake(column), slots], last_ss.at[i, k], last_rs.at[i, k], in_plane(to))

    for k in range(1, 4):
        last_zcopy(k).start()
    every(lambda k: last_copy(0, k, column_ahead(k), xy).start())
    for k in range(1, 4):
        for i in range(len(spans)):
            sum_copy(i, k).wait_send()
    for i in sent(ROUNDS - 1):
        wave_copy(ROUNDS - 1, i).wait_send()
    for k in range(1, 4):
        last_zcopy(k).wait_recv()
    every(lambda k: last_copy(1, k, column_ahead(k), xy).start())
    last[pl.ds(block, 1)] = last_z[...][None]
    every(lambda k: last_copy(0, k, xy, column_behind(k)).wait_recv())
    every(lambda k: last_copy(1, k, xy, column_behind(k)).wait_recv())

    def quarter(place, q):
        return last[place, pl.ds(rem(z - q + 4, 4), 1)][0]

    for pair in range(8):
        slabs = []
        for place in (2 * pair, 2 * pair + 1):
            west = unpacked(quarter(place, 0), quarter(place, 1))
            east = unpacked(quarter(place, 2), quarter(place, 3))
            slabs.append([jnp.concatenate([west[half], east[half]], axis=1) for half in range(2)])
        for layer in range(4):
            rows = slice(4 * (layer % 2), 4 * (layer % 2) + 4)
            out_ref[layer, 8 * pair : 8 * pair + 8, :] = jnp.concatenate(
                [slab[layer // 2][rows] for slab in slabs], axis=0
            )
    for k in range(1, 4):
        last_zcopy(k).wait_send()
    for i in range(2):
        every(lambda k: last_copy(i, k, column_ahead(k), xy).wait_send())


def per_device(snapshots, reflect, courant, lags, owners):
    depth, rows, columns = courant.shape
    lines = depth * rows
    dma = pltpu.SemaphoreType.DMA
    any_space = pl.BlockSpec(memory_space=pl.ANY)
    scalars = pl.BlockSpec(memory_space=pltpu.SMEM)
    return pl.pallas_call(
        kernel,
        out_shape=jax.ShapeDtypeStruct(courant.shape, F32),
        in_specs=[any_space, any_space, any_space, scalars, scalars],
        out_specs=pl.BlockSpec(memory_space=pltpu.VMEM),
        scratch_shapes=[
            pltpu.VMEM((256, 256), BF16), pltpu.VMEM((OFFSETS, 256, 256), BF16), pltpu.VMEM((4, 64, 256), F32), dma((3,)),
            pltpu.VMEM((16, 16, 256), BF16), pltpu.VMEM((16, 16, 256), BF16), dma((16,)), dma((16,)),
            pltpu.VMEM((16, OFFSETS, 16, 256), BF16), pltpu.VMEM((16, OFFSETS, 16, 256), BF16),
            dma((CHUNKS, 16)), dma((CHUNKS, 16)), dma,
            pltpu.VMEM((8, 128), jnp.int32), pltpu.VMEM((16, 8, 128), jnp.int32), pltpu.SMEM((16, 8, 128), jnp.int32),
            dma((16,)), dma((16,)), dma,
            pltpu.VMEM((4, 16, 128), F32), pltpu.VMEM((16, 128), F32), pltpu.VMEM((4, 16, 128), F32), dma((4,)), dma((4,)),
            pltpu.VMEM((4, 128, 128), BF16), pltpu.VMEM((3, 128, 128), BF16), dma((3,)), dma((3,)),
            pltpu.VMEM((128, 128), BF16), pltpu.VMEM((4, 128, 128), BF16), dma((4,)), dma((4,)),
            pltpu.VMEM((128, 128), F32), pltpu.VMEM((4, 64, 128), F32), dma((3,)), dma((3,)),
            pltpu.VMEM((2 * LAG + 1, 128, 256), F32),
            pltpu.VMEM((4, 128, 128), F32), pltpu.VMEM((3, 128, 128), F32), dma((5, 3)), dma((5, 3)),
            pltpu.VMEM((ROUNDS, 2, 16, 128), F32), pltpu.VMEM((ROUNDS, 4, 2, 16, 128), F32),
            pltpu.VMEM((ROUNDS - 1, len(FAR), 16, 128), F32), dma((ROUNDS, len(NEAR))), dma((ROUNDS, len(NEAR))),
            dma((ROUNDS - 1, 4)), dma((ROUNDS - 1, 4)),
            pltpu.VMEM((4, 8, 128), F32), dma((3,)), dma((3,)),
            pltpu.VMEM((16, 4, 8, 128), F32), dma((2, 16)), dma((2, 16)),
        ],
        compiler_params=pltpu.CompilerParams(
            collective_id=0, has_side_effects=True, vmem_limit_bytes=60 * 1024 * 1024
        ),
        name="born",
    )(
        snapshots.reshape(lines, columns),
        reflect.reshape(reflect.shape[0], lines, columns),
        courant,
        lags,
        owners,
    )


def solution(mesh):
    in_specs = (
        P("off", "dep", None, None),
        P("off", "dep", None, None),
        P("dep", None, None),
        P("off"),
        P(),
    )
    return jax.shard_map(
        per_device, mesh=mesh, in_specs=in_specs, out_specs=P("dep", None, None), check_vma=False
    )
```
